32 devices in a mesh: dp: 2 (over y), ctx: 4 (over x, core), exp: 4 (over z).
Axes of the slice: x: 2, y: 2, z: 4, core: 2. Of those that a mesh axis runs over, the one named last changes fastest.
Arguments:
- tokens: bfloat16 [2, 8, 1024, 1024], P(None, ('dp', 'exp'), 'ctx'), may hold values from -6 to 6
- routes: int32 [2, 8, 1024, 8], P(None, ('dp', 'exp'), 'ctx'), may hold values from 0 to 31, all different within a row
- cotangent: bfloat16 [2, 8, 1024, 1024], P(None, ('dp', 'exp'), 'ctx'), may hold values from -6 to 6
- norm_one: bfloat16 [1024], P(('dp', 'ctx')), may hold values from 0.5 to 1.5
- norm_two: bfloat16 [1024], P(('dp', 'ctx')), may hold values from 0.5 to 1.5
- w_query: bfloat16 [1024, 1024], P(('dp', 'ctx')), may hold values from -0.5 to 0.5
- w_key: bfloat16 [1024, 512], P(('dp', 'ctx')), may hold values from -0.5 to 0.5
- w_value: bfloat16 [1024, 512], P(('dp', 'ctx')), may hold values from -0.1875 to 0.1875
- w_out: bfloat16 [1024, 1024], P(('dp', 'ctx')), may hold values from -9.4375 to 9.4375
- w_router: bfloat16 [1024, 32], P(('dp', 'ctx')), may hold values from -0.09375 to 0.09375
- w_gate: bfloat16 [32, 1024, 512], P('exp', ('dp', 'ctx')), may hold values from -0.1875 to 0.1875
- w_up: bfloat16 [32, 1024, 512], P('exp', ('dp', 'ctx')), may hold values from -0.1875 to 0.1875
- w_down: bfloat16 [32, 512, 1024], P('exp', None, ('dp', 'ctx')), may hold values from -4.71875 to 4.71875
Outputs:
- layer_out: bfloat16 [2, 8, 1024, 1024], P(None, ('dp', 'exp'), 'ctx')
- input_grad: bfloat16 [2, 8, 1024, 1024], P(None, ('dp', 'exp'), 'ctx')
- norm_one_grad: float32 [1024], P(('dp', 'ctx'))
- norm_two_grad: float32 [1024], P(('dp', 'ctx'))
- query_grad: float32 [1024, 1024], P(('dp', 'ctx'))
- key_grad: float32 [1024, 512], P(('dp', 'ctx'))
- value_grad: float32 [1024, 512], P(('dp', 'ctx'))
- out_grad: float32 [1024, 1024], P(('dp', 'ctx'))
- router_grad: float32 [1024, 32], P(('dp', 'ctx'))
- gate_grad: float32 [32, 1024, 512], P('exp', ('dp', 'ctx'))
- up_grad: float32 [32, 1024, 512], P('exp', ('dp', 'ctx'))
- down_grad: float32 [32, 512, 1024], P('exp', None, ('dp', 'ctx'))
The draws below stay inside these ranges and needn't reach their ends.
Inputs may be any that keep to these rules, and one draw needn't show every extreme that they name: `routes`: each token names 8 different experts.
All inputs are finite; a program needn't handle non-finite values.
Results may differ from the reference program's by a relative error of at most 0.024.
Values may be sent and summed in bfloat16 or wider, within the bound.
No kernel may reach another device: no remote copies, remote signals or barrier semaphores. Data moves between devices by JAX's collectives and lax.ppermute only.
A program may use at most 192 MiB of HBM per device.

```python
import jax
import jax.numpy as jnp
from jax import lax

D = 1024
H = 16
KVH = 8
HD = 64
EXPERTS = 32
FF = 512
TOPK = 8
BLOCK = 256
MICRO = 2
T_DEV = 256
L = 1024
NSEQ = 8
CAP = 72
N_CTX = 4


def level_of(stream_key, shape, cuts, smallest, top_value):
    def one(position, shards_of):
        heights = jax.random.uniform(jax.random.fold_in(jax.random.fold_in(stream_key, 6), position), (shards_of,), jnp.float32, smallest / len(cuts), top_value / len(cuts))
        return jnp.repeat(jnp.exp(heights), shape[position] // shards_of).reshape((-1,) + (1,) * (len(shape) - position - 1))

    factor_of = one(*cuts[0])
    for cut in cuts[1:]:
        factor_of = factor_of * one(*cut)
    return factor_of


def different_ones(stream_key, rows, count, top, lift):
    ranking = jax.random.permutation(jax.random.fold_in(stream_key, 1), count)
    favour = ranking
    for power in range(3):
        favour = favour * favour // count
    favour = favour * lift // count
    chance = jax.random.randint(jax.random.fold_in(stream_key, 2), (rows, count), 0, 4096) + favour
    sure = jax.random.permutation(jax.random.fold_in(stream_key, 3), rows)[jnp.arange(count) % rows]
    chance = jnp.where(jnp.arange(rows)[:, None] == sure[None, :], 1 << 14, chance)
    priority = chance * count + jnp.arange(count)
    return lax.top_k(priority.astype(jnp.int32), top)[1].astype(jnp.int32)


def gaussian(own_key, dims, scale, bound, split=(), kind=jnp.bfloat16):
    values = scale * jax.random.normal(own_key, dims, jnp.float32)
    if split:
        values = values * level_of(own_key, dims, split, -0.22, 0.18)
    return jnp.clip(values, -bound, bound).astype(kind)


def setup_inputs(seed: int = 0) -> dict:
    streams_of = jax.random.split(jax.random.key(seed), 14)
    return {
        "tokens": gaussian(streams_of[0], (MICRO, NSEQ, L, D), 1.0, 6.0, ((1, 8), (2, 4))),
        "routes": different_ones(streams_of[1], MICRO * NSEQ * L, EXPERTS, TOPK, 2048).reshape((MICRO, NSEQ, L, TOPK)),
        "cotangent": gaussian(streams_of[2], (MICRO, NSEQ, L, D), 1.0, 6.0, ((1, 8), (2, 4))),
        "norm_one": jnp.clip(1.0 + 0.1 * jax.random.normal(streams_of[3], (D,), jnp.float32), 0.5, 1.5).astype(jnp.bfloat16),
        "norm_two": jnp.clip(1.0 + 0.1 * jax.random.normal(streams_of[4], (D,), jnp.float32), 0.5, 1.5).astype(jnp.bfloat16),
        "w_query": gaussian(streams_of[5], (D, H * HD), (D // 8) ** -0.5, 0.5, ((0, 8),)),
        "w_key": gaussian(streams_of[6], (D, KVH * HD), (D // 8) ** -0.5, 0.5, ((0, 8),)),
        "w_value": gaussian(streams_of[7], (D, KVH * HD), D ** -0.5, 0.1875, ((0, 8),)),
        "w_out": gaussian(streams_of[8], (H * HD, D), (1 / (max(1, 8192 // L) * 0.05) ** 0.5), 9.4375, ((0, 8),)),
        "w_router": gaussian(streams_of[9], (D, EXPERTS), (4 * D) ** -0.5, 0.09375, ((0, 8),)),
        "w_gate": gaussian(streams_of[10], (EXPERTS, D, FF), D ** -0.5, 0.1875, ((0, 4), (1, 8))),
        "w_up": gaussian(streams_of[11], (EXPERTS, D, FF), D ** -0.5, 0.1875, ((0, 4), (1, 8))),
        "w_down": gaussian(streams_of[12], (EXPERTS, FF, D), (1 / (FF // 16 * 0.05) ** 0.5), 4.71875, ((0, 4), (2, 8))),
    }


EPSILON = 1e-06
BASE_THETA = 10000.0
NEGATIVE = -1e+30
ATTENTION_MULT = 0.015625
RESIDUAL_MULT = 0.22

@jax.custom_vjp
def low(v):
    return lax.optimization_barrier(v.astype(jnp.bfloat16)).astype(jnp.float32)

@jax.custom_vjp
def low_back(v):
    return v

def low_keep(v):
    return (low(v), None)

def low_pass(kept, grad):
    return (grad,)

def back_keep(v):
    return (v, None)

def back_low(kept, grad):
    return (low(grad),)
low.defvjp(low_keep, low_pass)
low_back.defvjp(back_keep, back_low)

def product(left, right):
    return jnp.dot(left, right, precision=lax.Precision.HIGHEST, preferred_element_type=jnp.float32)

def rotation(offset, row_count, head_size):
    half_size = head_size // 2
    inverse = jnp.exp(jnp.arange(half_size, dtype=jnp.float32) * (-2.0 * jnp.log(jnp.float32(BASE_THETA)) / head_size))
    places = (offset + jnp.arange(row_count, dtype=jnp.int32)).astype(jnp.float32)
    angles = places[:, None] * inverse[None, :]
    return (jnp.cos(angles), jnp.sin(angles))

def rotate(tensor, cosine, sine, forward):
    half_size = tensor.shape[-1] // 2
    former = tensor[..., :half_size]
    latter = tensor[..., half_size:]
    cosine = cosine[:, None, :]
    sine = sine[:, None, :] if forward else -sine[:, None, :]
    return jnp.concatenate([former * cosine - latter * sine, latter * cosine + former * sine], -1)

def normalize(values):
    factor = lax.rsqrt(lax.optimization_barrier(jnp.mean(values * values, -1, keepdims=True)) + EPSILON)
    return (values * factor, factor)

def reference(tokens, routes, cotangent, norm_one, norm_two, w_query, w_key, w_value, w_out, w_router, w_gate, w_up, w_down):
    cosine, sine = rotation(0, L, HD)
    group_size = H // KVH
    expert_slots = EXPERTS * CAP
    block_rows = min(512, L)
    score_scale = ATTENTION_MULT
    key_ids = jnp.arange(L, dtype=jnp.int32) // BLOCK
    route_blocks = routes.reshape(MICRO * NSEQ * N_CTX, T_DEV, TOPK)

    def attend(query_rot, key_rot, value_rows):

        def one_block(first_row):
            query_part = lax.dynamic_slice_in_dim(query_rot, first_row, block_rows, 0).reshape(block_rows, KVH, group_size, HD)
            raw_scores = jnp.einsum('qkgd,tkd->kgqt', query_part, key_rot, precision=lax.Precision.HIGHEST) * score_scale
            raw_scores = low_back(raw_scores)
            query_ids = (first_row + jnp.arange(block_rows, dtype=jnp.int32)) // BLOCK
            allowed = key_ids[None, :] <= query_ids[:, None]
            scores = jnp.where(allowed, raw_scores, NEGATIVE)
            row_top = lax.optimization_barrier(jnp.max(scores, -1, keepdims=True))
            expo = jnp.exp(scores - row_top)
            probs = low(expo / lax.optimization_barrier(jnp.sum(expo, -1, keepdims=True)))
            mixed = jnp.einsum('kgqt,tkd->qkgd', probs, value_rows, precision=lax.Precision.HIGHEST)
            return mixed.reshape(block_rows, H * HD)
        starts = (jnp.arange(L // block_rows, dtype=jnp.int32) * block_rows).astype(jnp.int32)
        return lax.map(jax.checkpoint(one_block), starts).reshape(L, H * HD)

    def layer(inputs, gain_one, gain_two, query_full, key_full, value_full, out_full, router_full, gate_full, up_full, down_full):

        def attention_part(sequence):
            normed_one, factor_one = normalize(sequence)
            normed_in = low(normed_one * gain_one)
            query_pre = low_back(product(normed_in, query_full))
            key_pre = low_back(product(normed_in, key_full))
            value_pre = low_back(product(normed_in, value_full))
            query_rot = low(rotate(query_pre.reshape(L, H, HD), cosine, sine, True))
            key_rot = low(rotate(key_pre.reshape(L, KVH, HD), cosine, sine, True))
            value_rows = low(value_pre).reshape(L, KVH, HD)
            attended = attend(query_rot, key_rot, value_rows)
            attended_low = low(low_back(attended))
            return sequence + RESIDUAL_MULT * low_back(product(attended_low, out_full))
        hidden = lax.map(jax.checkpoint(attention_part), inputs.reshape(MICRO * NSEQ, L, D))

        def expert_part(packed):
            hidden_rows, chosen = packed
            normed_two, factor_two = normalize(hidden_rows)
            moe_in = low(normed_two * gain_two)
            logits = low_back(product(moe_in, router_full))
            selected = jnp.take_along_axis(logits, chosen, 1)
            gate_probs = jax.nn.softmax(selected, -1)
            chosen_flat = chosen.reshape(T_DEV * TOPK).astype(jnp.int32)
            one_hot = (chosen_flat[:, None] == jnp.arange(EXPERTS, dtype=jnp.int32)[None, :]).astype(jnp.int32)
            before = jnp.cumsum(one_hot, 0, dtype=jnp.int32) - one_hot
            pair_rank = lax.optimization_barrier(jnp.sum(before * one_hot, -1, dtype=jnp.int32))
            slot_index = jnp.where(pair_rank < CAP, chosen_flat * CAP + pair_rank, expert_slots).astype(jnp.int32)
            pair_rows = jnp.repeat(moe_in, TOPK, axis=0)
            buffer = jnp.zeros((expert_slots + 1, D), jnp.float32).at[slot_index].set(pair_rows)
            expert_in = low_back(buffer[:expert_slots].reshape(EXPERTS, CAP, D))
            gate_h = low_back(jnp.einsum('ecd,edf->ecf', expert_in, gate_full, precision=lax.Precision.HIGHEST))
            up_h = low_back(jnp.einsum('ecd,edf->ecf', expert_in, up_full, precision=lax.Precision.HIGHEST))
            hidden_low = low(jax.nn.silu(gate_h) * up_h)
            expert_out = low(low_back(jnp.einsum('ecf,efd->ecd', hidden_low, down_full, precision=lax.Precision.HIGHEST)))
            table = jnp.concatenate([expert_out.reshape(expert_slots, D), jnp.zeros((1, D), jnp.float32)], 0)
            pair_out = table[slot_index].reshape(T_DEV, TOPK, D)
            return hidden_rows + RESIDUAL_MULT * lax.optimization_barrier(jnp.sum(gate_probs[..., None] * pair_out, 1))
        mixed = lax.map(jax.checkpoint(expert_part), (hidden.reshape(MICRO * NSEQ * N_CTX, T_DEV, D), route_blocks))
        return mixed.reshape(MICRO, NSEQ, L, D)
    mixed, pullback = jax.vjp(layer, tokens.astype(jnp.float32), norm_one.astype(jnp.float32), norm_two.astype(jnp.float32), w_query.astype(jnp.float32), w_key.astype(jnp.float32), w_value.astype(jnp.float32), w_out.astype(jnp.float32), w_router.astype(jnp.float32), w_gate.astype(jnp.float32), w_up.astype(jnp.float32), w_down.astype(jnp.float32))
    grads = pullback(cotangent.astype(jnp.float32))
    return (mixed.astype(jnp.bfloat16), grads[0].astype(jnp.bfloat16), grads[1], grads[2], grads[3], grads[4], grads[5], grads[6], grads[7], grads[8], grads[9], grads[10])
```

```python
import jax
import jax.numpy as jnp
from jax import lax
from jax.experimental import pallas as pl
from jax.experimental.pallas import tpu as pltpu
from jax.sharding import PartitionSpec as P

H = 16
KVH = 8
HD = 64
EXPERTS = 32
FF = 512
TOPK = 8
BLOCK = 256
CAP = 72
GROUP = H // KVH

EPSILON = 1e-06
BASE_THETA = 10000.0
NEGATIVE = -1e30
ATTENTION_MULT = 0.015625
RESIDUAL_MULT = 0.22

PLANE = ("dp", "ctx")
BF = jnp.bfloat16
F32 = jnp.float32


def dot(left, right):
    return jnp.dot(left, right, preferred_element_type=F32)


def dot_tn(left, right):
    return lax.dot_general(left, right, (((0,), (0,)), ((), ())), preferred_element_type=F32)


def dot_nt(left, right):
    return lax.dot_general(left, right, (((1,), (1,)), ((), ())), preferred_element_type=F32)


def add(left, right):
    return left.astype(F32) + right.astype(F32)


def relative(blocks, index):
    count = len(blocks)
    bit = 1
    while bit < count:
        on = (index & bit) != 0
        blocks = [jnp.where(on, blocks[j ^ bit], blocks[j]) for j in range(count)]
        bit *= 2
    return blocks


def reorder(array, count, index, axis):
    return jnp.concatenate(relative(jnp.split(array, count, axis), index), axis)


def plane_swap(array, mask):
    count = lax.axis_size("dp") * lax.axis_size("ctx")
    return lax.ppermute(array, PLANE, [(i, i ^ mask) for i in range(count)])


def sibling(array):
    return plane_swap(array, 1)


def halves(array):
    return jnp.split(array, 2, -2)


def gather_chips(own):
    chips = lax.axis_size("dp") * lax.axis_size("ctx") // 2
    if chips == 4:
        along_x, along_y = plane_swap(own, 2), plane_swap(own, 4)
        first, last = halves(along_x)[0], halves(along_y)[1]
        far = jnp.concatenate([plane_swap(first, 4), plane_swap(last, 2)], -2)
        return [own, along_x, along_y, far]
    blocks, mask = [own], 1
    while mask < chips:
        blocks = blocks + [plane_swap(b, 2 * mask) for b in blocks]
        mask *= 2
    return blocks


def gather_plane(own):
    blocks = []
    for block in gather_chips(own):
        blocks += [block, sibling(block)]
    return blocks


def reduce_chips(blocks):
    chips = len(blocks)
    if chips == 4:
        upper, lower = zip(*[halves(b) for b in blocks])
        from_x = plane_swap(jnp.concatenate([upper[1], upper[3]], -2), 2)
        from_y = plane_swap(jnp.concatenate([lower[2], lower[3]], -2), 4)
        x_own, x_rest = halves(from_x)
        y_own, y_rest = halves(from_y)
        upper_last = plane_swap(add(upper[2], x_rest).astype(BF), 4)
        lower_last = plane_swap(add(lower[1], y_rest).astype(BF), 2)
        top = add(upper[0], x_own) + upper_last.astype(F32)
        low = add(lower[0], y_own) + lower_last.astype(F32)
        return jnp.concatenate([top, low], -2)
    mask = chips // 2
    while mask:
        blocks = [
            add(blocks[j], plane_swap(blocks[j + mask], 2 * mask)).astype(BF) for j in range(mask)
        ]
        mask //= 2
    return blocks[0].astype(F32)


def reduce_plane(blocks):
    other = sibling(jnp.concatenate(blocks[1::2], -2))
    others = jnp.split(other, len(blocks) // 2, -2)
    return reduce_chips([add(a, b).astype(BF) for a, b in zip(blocks[0::2], others)])


def gather_ctx(own):
    count = lax.axis_size("ctx")
    if count == 4:
        near = lax.ppermute(own, "ctx", [(0, 1), (2, 3)])
        along = lax.ppermute(own, "ctx", [(0, 2), (1, 3)])
        far = lax.ppermute(along, "ctx", [(2, 3), (3, 2)])
        return [own, near, along, far]
    blocks, mask = [own], 1
    while mask < count:
        blocks = blocks + [
            lax.ppermute(b, "ctx", [(i, i ^ mask) for i in range(count)]) for b in blocks
        ]
        mask *= 2
    return blocks


def reduce_ctx(blocks):
    count = lax.axis_size("ctx")
    if count == 4:
        far = lax.ppermute(blocks[3], "ctx", [(2, 3), (3, 2)])
        along = lax.ppermute(add(blocks[2], far).astype(BF), "ctx", [(2, 0), (3, 1)])
        near = lax.ppermute(blocks[1], "ctx", [(1, 0), (3, 2)])
        return add(blocks[0], near) + along.astype(F32)
    mask = count // 2
    while mask:
        perm = [(i, i ^ mask) for i in range(count)]
        blocks = [
            add(blocks[j], lax.ppermute(blocks[j + mask], "ctx", perm)).astype(BF)
            for j in range(mask)
        ]
        mask //= 2
    return blocks[0].astype(F32)


def ring_step(array):
    count = lax.axis_size("exp")
    return lax.ppermute(array, "exp", [(i, (i + 1) % count) for i in range(count)])


def gather_ring(own):
    blocks = [own]
    for _ in range(lax.axis_size("exp") - 1):
        blocks.append(ring_step(blocks[-1]))
    return blocks


def reduce_ring(blocks):
    count = len(blocks)
    total = blocks[1 % count]
    for k in range(2, count + 1):
        total = add(ring_step(total), blocks[k % count]).astype(BF)
    return total


def rotation(offset, row_count):
    half_size = HD // 2
    inverse = jnp.exp(jnp.arange(half_size, dtype=F32) * (-2.0 * jnp.log(F32(BASE_THETA)) / HD))
    places = (offset + jnp.arange(row_count, dtype=jnp.int32)).astype(F32)
    angles = places[:, None] * inverse[None, :]
    return (jnp.cos(angles), jnp.sin(angles))


def rope(pair, cosine, sine):
    lane = lax.broadcasted_iota(jnp.int32, pair.shape, 1)
    former = lane % HD < HD // 2
    turned = jnp.where(
        former, pltpu.roll(pair, 2 * HD - HD // 2, 1), pltpu.roll(pair, HD // 2, 1)
    )
    return pair * cosine + turned * sine


def inverse_rms(values):
    return lax.rsqrt(jnp.mean(values * values, -1, keepdims=True) + EPSILON)


def spec(shape, index=None):
    index = index or (lambda *_: (0,) * len(shape))
    return pl.BlockSpec(shape, index)


def once(shape, index=None):
    index = index or (lambda *_: (0,) * len(shape))
    return pl.BlockSpec(shape, index, pipeline_mode=pl.Buffered(1))


def smem():
    return pl.BlockSpec(memory_space=pltpu.SMEM)


def shape_of(shape, kind):
    return jax.ShapeDtypeStruct(shape, kind)


def call(
    body, grid, in_specs, out_specs, out_shape, scratch, args, flops, moved, limit=56, after=()
):
    count, first = len(after), len(args)

    def ordered(*refs):
        body(*refs[:first], *refs[first + count :])

    return pl.pallas_call(
        ordered,
        grid=grid,
        in_specs=list(in_specs) + [pl.BlockSpec(memory_space=pl.ANY)] * count,
        out_specs=out_specs,
        out_shape=out_shape,
        scratch_shapes=scratch,
        compiler_params=pltpu.CompilerParams(vmem_limit_bytes=limit << 20),
        cost_estimate=pl.CostEstimate(flops=flops, bytes_accessed=moved, transcendentals=0),
    )(*args, *after)


def lanes(index, size):
    return pl.ds(pl.multiple_of(index * size, size), size)


def fill(scratch, shards, rows):
    for j in range(shards.shape[0]):
        scratch[j * rows : (j + 1) * rows, :] = shards[j, :rows, :]


def prepare(index, routes, cotangent, chips):
    micro, rows, width = cotangent.shape
    part = width // chips

    def body(index_ref, routes_ref, cotangent_ref, picks_ref, *messages):
        chip = index_ref[0]
        earlier = lax.broadcasted_iota(jnp.int32, (rows, rows), 0) > lax.broadcasted_iota(
            jnp.int32, (rows, rows), 1
        )
        earlier = jnp.where(earlier, 1.0, 0.0).astype(BF)
        expert = lax.broadcasted_iota(jnp.int32, (rows, 128), 1)
        for m in range(micro):
            chosen = routes_ref[m]
            pick = jnp.zeros((rows, 128), F32)
            for k in range(TOPK):
                pick = pick + jnp.where(chosen[:, k : k + 1] == expert, 1.0, 0.0)
            rank = dot(earlier, pick.astype(BF))
            slot = jnp.where((pick > 0.0) & (rank < CAP), rank, -1.0).T
            picks_ref[m] = pick
            out = messages[m]
            for j in range(chips):
                out[:rows, j * part : (j + 1) * part] = cotangent_ref[m, :, lanes(j ^ chip, part)]
            out[rows:, :] = jnp.concatenate(
                [slot[:16], slot[16:32], jnp.zeros((16, width - 2 * rows), F32)], 1
            ).astype(BF)

    message = (rows + 16, width)
    return call(
        body,
        (1,),
        [smem(), spec(routes.shape), spec(cotangent.shape)],
        [spec((micro, rows, 128))] + [spec(message)] * micro,
        [shape_of((micro, rows, 128), F32)] + [shape_of(message, BF)] * micro,
        [],
        (index, routes, cotangent),
        1 << 26,
        4 << 20,
    )


def project(tokens, first, gain, cosine, sine, after=()):
    micro, rows, width = tokens.shape
    shard = width // first.shape[0]
    columns = first.shape[2]
    queries, keys = H * HD, KVH * HD

    def body(tokens_ref, first_ref, gain_ref, cosine_ref, sine_ref, normed_ref, query_ref, *rest):
        kv_refs, weight = rest[:micro], rest[micro]
        fill(weight, first_ref, shard)
        cos, sin = cosine_ref[...], sine_ref[...]
        for m in range(micro):
            values = tokens_ref[m].astype(F32)
            normed = (values * inverse_rms(values) * gain_ref[...]).astype(BF)
            normed_ref[m * rows : (m + 1) * rows, :] = normed
            for j in range(queries // 256):
                got = dot(normed, weight[:, j * 256 : (j + 1) * 256])
                for i in range(2):
                    turned = rope(got[:, i * 128 : (i + 1) * 128], cos, sin)
                    at = j * 256 + i * 128
                    query_ref[m, :, at : at + 128] = turned.astype(BF)
            for j in range(keys // 256):
                got = dot(normed, weight[:, queries + j * 256 : queries + (j + 1) * 256])
                for i in range(2):
                    turned = rope(got[:, i * 128 : (i + 1) * 128], cos, sin)
                    at = j * 256 + i * 128
                    kv_refs[m][:, at : at + 128] = turned.astype(BF)
            got = dot(normed, weight[:, queries + keys :])
            kv_refs[m][:, keys:] = got.astype(BF)

    kv = (rows, 2 * keys)
    return call(
        body,
        (1,),
        [spec(a.shape) for a in (tokens, first, gain, cosine, sine)],
        [spec((micro * rows, width)), spec((micro, rows, queries))] + [spec(kv)] * micro,
        [shape_of((micro * rows, width), BF), shape_of((micro, rows, queries), BF)]
        + [shape_of(kv, BF)] * micro,
        [pltpu.VMEM((width, columns), BF)],
        (tokens, first, gain, cosine, sine),
        2 * micro * rows * width * columns,
        12 << 20,
        after=after,
    )


def place_heads(pair, which):
    lane = lax.broadcasted_iota(jnp.int32, pair.shape, 1)
    mine = (lane < HD) if which == 0 else (lane >= HD)
    moved = pltpu.roll(pair, HD, 1)
    both = (pair, moved) if which == 0 else (moved, pair)
    return jnp.concatenate([jnp.where(mine, b, 0.0) for b in both], 0)


def attend(index, query, blocks, after=()):
    rows = query.shape[0]
    count = len(blocks)
    steps = KVH // 2
    width = H * HD

    def body(index_ref, query_ref, *refs):
        key_refs, value_refs = refs[:count], refs[count : 2 * count]
        low_ref, turned_ref, stat_ref = refs[2 * count : 2 * count + 3]
        top, total, mixed = refs[2 * count + 3 :]
        ctx = index_ref[2]
        heads = []
        for a in range(2):
            pair = query_ref[:, a * 128 : (a + 1) * 128].astype(F32) * ATTENTION_MULT
            heads.append(place_heads(pair, a).T.astype(BF))

        def visit(j):
            key, value = key_refs[j][...], value_refs[j][...]
            for a in range(2):
                scores = dot(key, heads[a])
                peak = jnp.max(scores, 0, keepdims=True)
                if j:
                    peak = jnp.maximum(peak, top[a])
                expo = jnp.exp(scores - peak)
                added = jnp.sum(expo, 0, keepdims=True)
                got = dot_tn(value, expo.astype(BF))[a * HD : (a + 1) * HD]
                if j:
                    scale = jnp.exp(top[a] - peak)
                    added = added + total[a] * scale
                    got = got + mixed[a] * scale
                top[a] = peak
                total[a] = added
                mixed[a] = got

        visit(0)
        for j in range(1, count):
            pl.when((ctx ^ j) <= ctx)(lambda j=j: visit(j))
        for a in range(2):
            got = mixed[a] / total[a]
            turned = jnp.concatenate([got[:, :rows], got[:, rows:]], 0)
            turned_ref[a * 128 : (a + 1) * 128, :] = turned
            low_ref[:, a * 128 : (a + 1) * 128] = turned.T.astype(BF)
            stat_ref[0, a : a + 1, :] = top[a] + jnp.log(total[a])

    keys = [spec((rows, 128), lambda i: (0, i))] * count
    values = [spec((rows, 128), lambda i: (0, i + steps))] * count
    return call(
        body,
        (steps,),
        [smem(), spec((rows, 256), lambda i: (0, i))] + keys + values,
        [
            spec((rows, 256), lambda i: (0, i)),
            spec((256, rows), lambda i: (i, 0)),
            spec((1, 2, 2 * rows), lambda i: (i, 0, 0)),
        ],
        [
            shape_of((rows, width), BF),
            shape_of((width, rows), F32),
            shape_of((steps, 2, 2 * rows), F32),
        ],
        [
            pltpu.VMEM((2, 1, 2 * rows), F32),
            pltpu.VMEM((2, 1, 2 * rows), F32),
            pltpu.VMEM((2, HD, 2 * rows), F32),
        ],
        (index, query, *blocks, *blocks),
        8 * rows * rows * count * width,
        6 << 20,
        after=after,
    )


def attend_back(index, query, blocks, attended_grad, attended, stats, cosine, sine, after=()):
    rows = query.shape[0]
    count = len(blocks)
    steps = KVH // 2
    half = HD // 2

    def body(index_ref, query_ref, grad_ref, attended_ref, stat_ref, cosine_ref, sine_ref, *refs):
        key_refs, value_refs = refs[:count], refs[count : 2 * count]
        query_out, kv_out = refs[2 * count], refs[2 * count + 1 : 3 * count + 1]
        (query_sum,) = refs[3 * count + 1 :]
        ctx = index_ref[2]
        step = pl.program_id(0)
        heads, grads, heads_t, grads_t, deltas = [], [], [], [], []
        for a in range(2):
            at = slice(a * 128, (a + 1) * 128)
            placed = place_heads(query_ref[:, at].astype(F32) * ATTENTION_MULT, a)
            heads.append(placed.astype(BF))
            heads_t.append(placed.T.astype(BF))
            pair = grad_ref[:, at].astype(F32)
            placed = place_heads(pair, a)
            grads.append(placed.astype(BF))
            grads_t.append(placed.T.astype(BF))
            product = pair.T * attended_ref[at, :]
            deltas.append(
                jnp.concatenate(
                    [jnp.sum(product[i * HD : (i + 1) * HD], 0, keepdims=True) for i in range(2)], 1
                )
            )

        def visit(j):
            key, value = key_refs[j][...], value_refs[j][...]
            key_sum, value_sum = 0.0, 0.0
            for a in range(2):
                probs = jnp.exp(dot(key, heads_t[a]) - stat_ref[0, a : a + 1, :])
                score_grad = (probs * (dot(value, grads_t[a]) - deltas[a])).astype(BF)
                key_sum = key_sum + dot(score_grad, heads[a])
                value_sum = value_sum + dot(probs.astype(BF), grads[a])
                got = dot_tn(key, score_grad)[a * HD : (a + 1) * HD]
                if j:
                    got = got + query_sum[a]
                query_sum[a] = got
            kv_out[j][:, lanes(step, 128)] = key_sum.astype(BF)
            kv_out[j][:, lanes(step + steps, 128)] = value_sum.astype(BF)

        visit(0)
        for j in range(1, count):
            reach = (ctx ^ j) <= ctx
            pl.when(reach)(lambda j=j: visit(j))

            @pl.when(jnp.logical_not(reach) & (step == 0))
            def _(j=j):
                kv_out[j][...] = jnp.zeros_like(kv_out[j])

        cos, sin = cosine_ref[...], sine_ref[...]
        for a in range(2):
            got = query_sum[a] * ATTENTION_MULT
            pieces = []
            for i in range(2):
                former = got[:half, i * rows : (i + 1) * rows]
                latter = got[half:, i * rows : (i + 1) * rows]
                pieces += [former * cos + latter * sin, latter * cos - former * sin]
            query_out[:, a * 128 : (a + 1) * 128] = jnp.concatenate(pieces, 0).T.astype(BF)

    wide = spec((rows, 256), lambda i: (0, i))
    keys = [spec((rows, 128), lambda i: (0, i))] * count
    values = [spec((rows, 128), lambda i: (0, i + steps))] * count
    kv = (rows, 2 * KVH * HD)
    return call(
        body,
        (steps,),
        [
            smem(),
            wide,
            wide,
            spec((256, rows), lambda i: (i, 0)),
            spec((1, 2, 2 * rows), lambda i: (i, 0, 0)),
            spec(cosine.shape),
            spec(sine.shape),
        ]
        + keys
        + values,
        [wide] + [spec(kv)] * count,
        [shape_of((rows, H * HD), BF)] + [shape_of(kv, BF)] * count,
        [pltpu.VMEM((2, HD, 2 * rows), F32)],
        (index, query, attended_grad, attended, stats, cosine, sine, *blocks, *blocks),
        20 * rows * rows * count * H * HD,
        8 << 20,
        after=after,
    )


def route(index, attended, tokens, second, gain, router, picks, chips, after=()):
    rows, width = attended.shape
    shard = width // second.shape[0]
    part = width // chips

    def body(
        index_ref, attended_ref, tokens_ref, second_ref, gain_ref, router_ref, picks_ref,
        hidden_ref, moe_ref, probs_ref, message_ref, weight,
    ):
        chip = index_ref[0]
        fill(weight, second_ref, shard)
        hidden = tokens_ref[...].astype(F32) + RESIDUAL_MULT * dot(attended_ref[...], weight[...])
        hidden_ref[...] = hidden
        moe_in = (hidden * inverse_rms(hidden) * gain_ref[...]).astype(BF)
        moe_ref[...] = moe_in
        picked = picks_ref[...] > 0.0
        chosen = jnp.where(picked, dot(moe_in, router_ref[...]), NEGATIVE)
        expo = jnp.where(picked, jnp.exp(chosen - jnp.max(chosen, -1, keepdims=True)), 0.0)
        probs = expo / jnp.sum(expo, -1, keepdims=True)
        probs_ref[...] = probs
        for j in range(chips):
            message_ref[:rows, j * part : (j + 1) * part] = moe_ref[:, lanes(j ^ chip, part)]
        turned = probs.T
        high = turned.astype(BF).astype(F32)
        low = turned - high
        message_ref[rows:, :] = jnp.concatenate(
            [high[:16], high[16:32], low[:16], low[16:32]], 1
        ).astype(BF)

    return call(
        body,
        (1,),
        [smem()] + [spec(a.shape) for a in (attended, tokens, second, gain, router, picks)],
        [spec((rows, width)), spec((rows, width)), spec((rows, 128)), spec((rows + 16, width))],
        [
            shape_of((rows, width), F32),
            shape_of((rows, width), BF),
            shape_of((rows, 128), F32),
            shape_of((rows + 16, width), BF),
        ],
        [pltpu.VMEM((width, width), BF)],
        (index, attended, tokens, second, gain, router, picks),
        2 * rows * width * width,
        6 << 20,
        after=after,
    )


def expert_row(ref, start, rows, expert, first):
    table = ref[start : start + 16, pl.ds(pl.multiple_of((expert // 16) * rows + first, rows), rows)]
    table = table.astype(F32)
    line = lax.broadcasted_iota(jnp.int32, table.shape, 0) == expert % 16
    return jnp.sum(jnp.where(line, table, 0.0), 0, keepdims=True)


def slots_of(row):
    slot = lax.broadcasted_iota(jnp.int32, (CAP, row.shape[1]), 0).astype(F32)
    return jnp.where(slot == row, 1.0, 0.0)


def experts(index, offset, token_blocks, grad_blocks, gate_up, down, after=()):
    runs = len(token_blocks)
    rows, width = token_blocks[0].shape[0] - 16, token_blocks[0].shape[1]
    count = gate_up[0].shape[0]
    slots = runs * CAP
    part = width // len(gate_up) if len(gate_up) != 5 else width // 4
    pieces = len(gate_up)

    def body(index_ref, *refs):
        tokens_in, grads_in = refs[:runs], refs[runs : 2 * runs]
        at = 2 * runs
        gate_up_in, down_in = refs[at : at + pieces], refs[at + pieces : at + 2 * pieces]
        at += 2 * pieces
        received_ref, pair_ref, inner_ref, hidden_ref, out_ref, back_ref, sens_ref = refs[at : at + 7]
        received, grads, weights, wide, deep = refs[at + 7 :]
        step = pl.program_id(0)

        @pl.when(step == 0)
        def _():
            for k in range(0, runs, 2):
                found = []
                for r in (k, k + 1):
                    takes, probs = [], []
                    for i in range(count):
                        expert = index_ref[3] + offset + i
                        take = slots_of(expert_row(grads_in[r], rows, rows, expert, 0))
                        prob = expert_row(tokens_in[r], rows, rows, expert, 0) + expert_row(
                            tokens_in[r], rows, rows, expert, 2 * rows
                        )
                        takes.append(take)
                        probs.append(jnp.sum(take * prob, 1, keepdims=True))
                    take = jnp.concatenate(takes, 0).astype(BF)
                    found.append(
                        (dot(take, tokens_in[r][:rows, :]), dot(take, grads_in[r][:rows, :]), probs)
                    )
                for i in range(count):
                    span = slice(k * CAP, (k + 2) * CAP)
                    pick = slice(i * CAP, (i + 1) * CAP)
                    received[i, span, :] = jnp.concatenate([f[0][pick] for f in found], 0).astype(BF)
                    grads[i, span, :] = jnp.concatenate([f[1][pick] for f in found], 0).astype(BF)
                    prob = jnp.concatenate([f[2][i] for f in found], 0)
                    weights[i, span, :] = jnp.broadcast_to(prob, (2 * CAP, 128))

        if pieces == 5:
            for j in range(3):
                wide[j * part : (j + 1) * part, :] = gate_up_in[j][0]
                deep[:, j * part : (j + 1) * part] = down_in[j][0]
            wide[3 * part : 3 * part + part // 2, :] = gate_up_in[3][0]
            wide[3 * part + part // 2 :, :] = gate_up_in[4][0]
            deep[: FF // 2, 3 * part :] = down_in[3][0]
            deep[FF // 2 :, 3 * part :] = down_in[4][0]
        else:
            for j in range(pieces):
                wide[j * part : (j + 1) * part, :] = gate_up_in[j][0]
                deep[:, j * part : (j + 1) * part] = down_in[j][0]

        rows_in = received[step]
        received_ref[0] = rows_in
        prob = weights[step][:, :1]
        scaled = RESIDUAL_MULT * grads[step].astype(F32)
        pair = (prob * scaled).astype(BF)
        pair_ref[0] = pair
        both = dot(rows_in, wide[...])
        gate_h, up_h = both[:, :FF], both[:, FF:]
        sigma = jax.nn.sigmoid(gate_h)
        silu_gate = gate_h * sigma
        hidden = (silu_gate * up_h).astype(BF)
        hidden_ref[0] = hidden
        inner = dot_nt(pair, deep[...])
        gate_d = (inner * up_h * sigma * (1.0 + gate_h * (1.0 - sigma))).astype(BF)
        up_d = (inner * silu_gate).astype(BF)
        inner_ref[0, :, :FF] = gate_d
        inner_ref[0, :, FF:] = up_d
        out = dot(hidden, deep[...]).astype(BF).astype(F32)
        out_ref[0] = (prob * out).astype(BF)
        sens = jnp.sum(out * scaled, 1, keepdims=True)
        expert = index_ref[3] + offset + step
        for r in range(runs):
            take = slots_of(expert_row(grads_in[r], rows, rows, expert, 0))
            sens_ref[0, r : r + 1, :] = jnp.sum(
                take * sens[r * CAP : (r + 1) * CAP], 0, keepdims=True
            )
        back_ref[0] = dot_nt(inner_ref[0], wide[...]).astype(BF)

    message = (rows + 16, width)
    step = lambda i: (i, 0, 0)
    sizes = [width, width, 2 * FF, FF, width, width]
    return call(
        body,
        (count,),
        [smem()]
        + [once(message)] * (2 * runs)
        + [spec((1,) + a.shape[1:], step) for a in gate_up]
        + [spec((1,) + a.shape[1:], step) for a in down],
        [spec((1, slots, n), step) for n in sizes] + [spec((1, runs, rows), step)],
        [shape_of((count, slots, n), BF) for n in sizes] + [shape_of((count, runs, rows), F32)],
        [
            pltpu.VMEM((count, slots, width), BF),
            pltpu.VMEM((count, slots, width), BF),
            pltpu.VMEM((count, slots, 128), F32),
            pltpu.VMEM((width, 2 * FF), BF),
            pltpu.VMEM((FF, width), BF),
        ],
        (index, *token_blocks, *grad_blocks, *gate_up, *down),
        count * slots * width * FF * 16,
        count * slots * 14 << 10,
        60,
        after,
    )


def grad_cuts(width, deep):
    part, half = width // 4, width // 8
    if not deep:
        def cut(j, lower):
            first = j * part + (half if lower else 0)
            return slice(first, first + half), slice(None)
        own = (slice(0, part), slice(None))
    else:
        def cut(j, lower):
            first = FF // 2 if lower else 0
            return slice(first, first + FF // 2), slice(j * part, (j + 1) * part)
        own = (slice(None), slice(0, part))
    return [
        [cut(1, False), cut(3, False)],
        [cut(2, True), cut(3, True)],
        [own],
        [cut(2, False)],
        [cut(1, True)],
    ]


def expert_grads(parts, after=()):
    count, slots, width = parts[0][0].shape
    full = [(width, 2 * FF), (FF, width)]
    cuts = [grad_cuts(width, deep) for deep in (False, True)]

    def extent(cut, size):
        return [len(range(n)[c]) for c, n in zip(cut, size)]

    shapes = []
    for size, pieces in zip(full, cuts):
        for piece in pieces:
            one = extent(piece[0], size)
            shapes.append((one[0] * len(piece), one[1]))

    def body(*refs):
        ins, outs = refs[: 4 * len(parts)], refs[4 * len(parts) :]
        received, pair, inner, hidden = [
            jnp.concatenate([ins[4 * p + i][0] for p in range(len(parts))], 0) for i in range(4)
        ]
        grads = dot_tn(received, inner).astype(BF), dot_tn(hidden, pair).astype(BF)
        at = 0
        for grad, pieces in zip(grads, cuts):
            for piece in pieces:
                row = 0
                for cut in piece:
                    value = grad[cut]
                    outs[at][0, row : row + value.shape[0], :] = value
                    row += value.shape[0]
                at += 1

    step = lambda i: (i, 0, 0)
    flat = [a for p in parts for a in p]
    got = call(
        body,
        (count,),
        [spec((1,) + a.shape[1:], step) for a in flat],
        [spec((1,) + n, step) for n in shapes],
        [shape_of((count,) + n, BF) for n in shapes],
        [],
        flat,
        len(parts) * count * slots * width * FF * 6,
        len(flat) * count * slots * 2 << 10,
        after=after,
    )
    return got[:5], got[5:]


def reduce_first(pieces):
    send_x, send_y, own, keep_y, keep_x = pieces
    x_own, x_rest = halves(plane_swap(send_x, 2))
    y_own, y_rest = halves(plane_swap(send_y, 4))
    return own, x_own, y_own, add(keep_y, x_rest).astype(BF), add(keep_x, y_rest).astype(BF)


def reduce_last(state):
    own, x_own, y_own, upper, lower = state
    from_y, from_x = plane_swap(upper, 4), plane_swap(lower, 2)
    top, low = halves(own)
    return jnp.concatenate([add(top, x_own) + from_y.astype(F32), add(low, y_own) + from_x.astype(F32)], -2)


def combine(index, grad_blocks, sources, senses=None, after=()):
    runs = len(grad_blocks)
    rows, width = grad_blocks[0].shape[0] - 16, grad_blocks[0].shape[1]
    chunks = len(sources)
    counts = [a.shape[0] for a in sources]
    steps = runs // 2
    total = sum(counts)
    senses = [a.reshape(a.shape[0], steps, 2, rows) for a in senses or ()]
    tall = rows + 16 if senses else rows

    def body(index_ref, *refs):
        slots_in, pairs_in = refs[:runs], refs[runs : runs + chunks]
        sens_in = refs[runs + chunks : runs + chunks + len(senses)]
        mine, *others = refs[runs + chunks + len(senses) :][: 1 + steps]
        table, choice = refs[runs + chunks + len(senses) + 1 + steps :]
        step = pl.program_id(0)
        first = index_ref[3]

        def fetch(k):
            for i in range(total):
                lines = [slots_of(expert_row(slots_in[2 * k + s], 0, rows, first + i, 0)) for s in range(2)]
                zero = jnp.zeros_like(lines[0])
                at = i * 2 * CAP
                choice[at : at + 2 * CAP, :] = jnp.concatenate(
                    [
                        jnp.concatenate([lines[0], zero], 1),
                        jnp.concatenate([zero, lines[1]], 1),
                    ],
                    0,
                ).astype(BF)

        for k in range(steps):
            pl.when(step == k)(lambda k=k: fetch(k))
        flat = jnp.concatenate(
            [a[...].reshape(n * 2 * CAP, width) for a, n in zip(pairs_in, counts)], 0
        )
        got = dot_tn(choice[...], flat).astype(BF)

        def put(s, first_row, last_row, value):
            if s == 0:
                mine[0, first_row:last_row, :] = value
                return
            for k in range(steps):

                @pl.when(step == k)
                def _(k=k):
                    others[k][first_row:last_row, :] = value

        for s in range(2):
            put(s, 0, rows, got[s * rows : (s + 1) * rows])
            if not senses:
                continue
            table[...] = jnp.zeros_like(table)
            i = 0
            for ref, n in zip(sens_in, counts):
                for e in range(n):
                    line = ref[e, 0, s : s + 1, :]
                    high = line.astype(BF).astype(F32)
                    expert = first + i
                    lane = (expert // 16) * rows
                    for value, base in ((high, 0), (line - high, 2 * rows)):
                        table[
                            pl.ds(expert % 16, 1), pl.ds(pl.multiple_of(lane + base, rows), rows)
                        ] = value
                    i += 1
            put(s, rows, rows + 16, table[...].astype(BF))

    return call(
        body,
        (steps,),
        [smem()]
        + [once((16, width), lambda k: (rows // 16, 0))] * runs
        + [spec((n, 2 * CAP, width), lambda k: (0, k, 0)) for n in counts]
        + [spec((a.shape[0], 1, 2, rows), lambda k: (0, k, 0, 0)) for a in senses],
        [spec((1, tall, width), lambda k: (k, 0, 0))] + [spec((tall, width))] * steps,
        [shape_of((steps, tall, width), BF)] + [shape_of((tall, width), BF)] * steps,
        [pltpu.VMEM((16, width), F32), pltpu.VMEM((total * 2 * CAP, 2 * rows), BF)],
        (index, *grad_blocks, *sources, *senses),
        4 * runs * total * CAP * rows * width,
        total * runs * CAP * width * 2,
        after=after,
    )


def hidden_back(
    index, total, hidden, gain, probs, cotangent, router, second, chips, after=()
):
    rows, width = hidden.shape
    shard = width // second.shape[0]
    part = width // chips

    def body(
        index_ref, total_ref, hidden_ref, gain_ref, probs_ref, cotangent_ref, router_ref, second_ref,
        hidden_grad_ref, branch_ref, attended_ref, logit_ref, norm_ref, weight,
    ):
        chip = index_ref[0]
        fill(weight, second_ref, shard)
        tail = total_ref[rows:, :].astype(F32)
        tail = tail[:, : 2 * rows] + tail[:, 2 * rows :]
        sens = jnp.concatenate(
            [tail[:, :rows], tail[:, rows:], jnp.zeros((128 - EXPERTS, rows), F32)], 0
        ).T
        probs = probs_ref[...]
        logit_grad = probs * (sens - jnp.sum(probs * sens, -1, keepdims=True))
        logit_grad = logit_grad.astype(BF)
        logit_ref[...] = logit_grad
        moved = jnp.concatenate(
            [total_ref[:rows, lanes(j ^ chip, part)] for j in range(chips)], 1
        ).astype(F32)
        moe_grad = moved + dot_nt(logit_grad, router_ref[...])
        hidden = hidden_ref[...]
        factor = inverse_rms(hidden)
        normed = hidden * factor
        norm_ref[...] = jnp.sum(moe_grad * normed, 0, keepdims=True)
        scaled = moe_grad * gain_ref[...]
        hidden_grad = cotangent_ref[...].astype(F32) + factor * (
            scaled - normed * jnp.mean(scaled * normed, -1, keepdims=True)
        )
        hidden_grad_ref[...] = hidden_grad
        branch = (RESIDUAL_MULT * hidden_grad).astype(BF)
        branch_ref[...] = branch
        attended_ref[...] = dot_nt(branch, weight[...]).astype(BF)

    args = (index, total, hidden, gain, probs, cotangent, router, second)
    return call(
        body,
        (1,),
        [smem()] + [spec(a.shape) for a in args[1:]],
        [spec((rows, width))] * 3 + [spec((rows, 128)), spec((1, width))],
        [
            shape_of((rows, width), F32),
            shape_of((rows, width), BF),
            shape_of((rows, width), BF),
            shape_of((rows, 128), BF),
            shape_of((1, width), F32),
        ],
        [pltpu.VMEM((width, width), BF)],
        args,
        2 * rows * width * width,
        8 << 20,
        after=after,
    )


def input_back(query_grad, kv_parts, tokens, first, gain, hidden_grad, cosine, sine, after=()):
    rows, width = tokens.shape
    shard = width // first.shape[0]
    columns = first.shape[2]
    queries, keys = H * HD, KVH * HD
    count = len(kv_parts)

    def body(query_ref, tokens_ref, first_ref, gain_ref, hidden_ref, cosine_ref, sine_ref, *refs):
        kv_refs = refs[:count]
        input_ref, low_ref, norm_ref, weight = refs[count:]
        fill(weight, first_ref, shard)
        cos, sin = cosine_ref[...], -sine_ref[...]
        low_ref[:, :queries] = query_ref[...]
        key = sum(r[:, :keys].astype(F32) for r in kv_refs)
        for j in range(keys // 128):
            turned = rope(key[:, j * 128 : (j + 1) * 128], cos, sin)
            low_ref[:, queries + j * 128 : queries + (j + 1) * 128] = turned.astype(BF)
        value = sum(r[:, keys:].astype(F32) for r in kv_refs)
        low_ref[:, queries + keys :] = value.astype(BF)
        sens = dot_nt(low_ref[...], weight[...])
        values = tokens_ref[...].astype(F32)
        factor = inverse_rms(values)
        normed = values * factor
        norm_ref[...] = jnp.sum(sens * normed, 0, keepdims=True)
        scaled = sens * gain_ref[...]
        input_ref[...] = (
            hidden_ref[...]
            + factor * (scaled - normed * jnp.mean(scaled * normed, -1, keepdims=True))
        ).astype(BF)

    args = (query_grad, tokens, first, gain, hidden_grad, cosine, sine, *kv_parts)
    return call(
        body,
        (1,),
        [spec(a.shape) for a in args],
        [spec((rows, width)), spec((rows, columns)), spec((1, width))],
        [shape_of((rows, width), BF), shape_of((rows, columns), BF), shape_of((1, width), F32)],
        [pltpu.VMEM((width, columns), BF)],
        args,
        2 * rows * width * columns,
        8 << 20,
        after=after,
    )


def on_device(
    tokens,
    routes,
    cotangent,
    norm_one,
    norm_two,
    w_query,
    w_key,
    w_value,
    w_out,
    w_router,
    w_gate,
    w_up,
    w_down,
):
    micro_count, _, rows, width = tokens.shape
    tokens, routes, cotangent = tokens[:, 0], routes[:, 0], cotangent[:, 0]
    local_experts, shard = w_gate.shape[0], w_gate.shape[1]
    core_experts = local_experts // 2
    ctx_count, exp_count = lax.axis_size("ctx"), lax.axis_size("exp")
    plane = lax.axis_size("dp") * ctx_count
    chips = plane // 2
    ctx = lax.axis_index("ctx")
    place = lax.axis_index("dp") * ctx_count + ctx
    chip, core = place // 2, place % 2
    first_expert = lax.axis_index("exp") * local_experts + core * core_experts
    index = jnp.stack([chip, core, ctx, first_expert]).astype(jnp.int32)
    micros = range(micro_count)

    cosine, sine = rotation(ctx * rows, rows)
    cosine_t, sine_t = cosine.T, sine.T
    cosine_w = jnp.tile(cosine, (1, 4))
    sine_w = jnp.concatenate([-sine, sine, -sine, sine], 1)

    gains = jnp.concatenate([norm_one, norm_two])[None, :]
    gains = jnp.pad(gains, ((0, 15), (0, w_query.shape[1] * 2 - gains.shape[1])))
    first_set = jnp.concatenate([jnp.concatenate([w_query, w_key, w_value], 1), gains], 0)
    router_rows = w_router.reshape(-1, width)
    router_count = router_rows.shape[0]
    router_rows = jnp.pad(router_rows, ((0, 16 - router_count), (0, 0)))
    second_set = jnp.concatenate([w_out, router_rows], 0)
    first = lax.all_gather(first_set, PLANE)
    second = lax.all_gather(second_set, PLANE)
    gain_one = first[:, shard, :shard].reshape(1, width).astype(F32)
    gain_two = first[:, shard, shard : 2 * shard].reshape(1, width).astype(F32)
    router = second[:, shard : shard + router_count].reshape(width, EXPERTS)
    router = jnp.pad(router, ((0, 0), (0, 128 - EXPERTS)))

    def later(array, *others):
        return lax.optimization_barrier((array,) + others)[0]

    class Ring:
        def __init__(self, message):
            self.blocks, self.siblings = [message], [sibling(message)]

        def step(self):
            self.blocks.append(ring_step(self.blocks[-1]))
            self.siblings.append(sibling(self.blocks[-1]))
            return self.blocks[-1]

        def runs(self):
            while len(self.blocks) < exp_count:
                self.step()
            return [b for pair in zip(self.blocks, self.siblings) for b in pair]

    class Home:
        def __init__(self, mine, others):
            self.got = [sibling(o) for o in others[1:] + others[:1]]
            self.got = self.got[-1:] + self.got[:-1]
            self.mine = mine
            self.at = 1
            self.total = add(mine[1], self.got[1]).astype(BF)

        def step(self):
            self.at += 1
            k = self.at % exp_count
            moved = ring_step(self.total).astype(F32)
            self.total = (moved + add(self.mine[k], self.got[k])).astype(BF)
            return self.total

        def end(self):
            while self.at < exp_count:
                self.step()
            return self.total

    def swap_in(array, axis):
        mine = lax.dynamic_slice_in_dim(array, core * core_experts, core_experts, 0)
        other = lax.dynamic_slice_in_dim(array, (1 - core) * core_experts, core_experts, 0)
        got = sibling(other)
        pair = [jnp.where(core == 0, mine, got), jnp.where(core == 0, got, mine)]
        return jnp.concatenate(pair, axis)

    def swap_out(array, axis):
        half = array.shape[axis] // 2
        mine = lax.dynamic_slice_in_dim(array, core * half, half, axis)
        other = lax.dynamic_slice_in_dim(array, (1 - core) * half, half, axis)
        got = sibling(other.astype(BF)).astype(F32)
        pair = [jnp.where(core == 0, mine, got), jnp.where(core == 0, got, mine)]
        return jnp.concatenate(pair, 0)

    def run_attention(m, after=()):
        low, turned, stats = attend(index, query[m], kv_blocks[m], after)
        return low, turned, stats

    def run_route(m, low, after=()):
        return route(
            index, low, tokens[m], second, gain_two, router, picks[m], chips, after
        )

    def run_hidden_back(m, in_total, after=()):
        return hidden_back(
            index, in_total, hidden[m], gain_two, probs[m], cotangent[m], router, second, chips, after
        )

    def run_attend_back(m, attended_grad, after=()):
        return attend_back(
            index, query[m], kv_blocks[m], attended_grad, turned[m], stats[m], cosine_t, sine_t, after
        )

    def run_input_back(m, query_grad, kv_parts, hidden_grad, after=()):
        return input_back(
            query_grad, kv_parts, tokens[m], first, gain_one, hidden_grad, cosine_w, sine_w, after
        )

    def finish_output(m, total):
        rows_out = reorder(total, chips, chip, 1).astype(F32)
        return (hidden[m] + RESIDUAL_MULT * rows_out).astype(BF)

    picks, *messages = prepare(index, routes, cotangent, chips)
    g_rings = [Ring(message) for message in messages]
    gate_up_own = swap_in(jnp.concatenate([w_gate, w_up], 2), 1)
    down_own = swap_in(w_down, 2)
    attended_low, turned, stats, hidden, moe_in, probs = [[None] * micro_count for _ in range(6)]
    backs, outputs = [None] * micro_count, [None] * micro_count

    if chips == 4 and exp_count == 4 and ctx_count == 4 and micro_count == 2 and core_experts % 2 == 0:
        half = core_experts // 2

        class Weights:
            def __init__(self, c, *after):
                self.near = []
                for array in (gate_up_own, down_own):
                    own = later(array[c * half : (c + 1) * half], *after)
                    self.near.append((own, plane_swap(own, 2), plane_swap(own, 4)))

            def hand_on(self):
                self.parts = [(halves(x)[0], halves(y)[1]) for _, x, y in self.near]
                return tuple(a for pair in self.parts for a in pair)

            def full(self):
                return [
                    near + (plane_swap(a, 4), plane_swap(b, 2))
                    for near, (a, b) in zip(self.near, self.parts)
                ]

        def one_experts(c, m, full, after):
            return experts(index, c * half, x_rings[m].runs(), g_rings[m].runs(), *full, after=after)

        def gather_near(kv):
            near = lax.ppermute(kv, "ctx", [(0, 1), (2, 3)])
            along = lax.ppermute(kv, "ctx", [(0, 2), (1, 3)])
            far = lax.ppermute(along, "ctx", [(2, 3), (3, 2)])
            return [kv, near, along, far]

        g_steps = [ring.step() for ring in g_rings]
        normed_in, query, *kv_own = project(tokens, first, gain_one, cosine_w, sine_w, g_steps)
        g_steps = [ring.step() for ring in g_rings]
        kv_blocks = [gather_near(kv) for kv in kv_own]
        early = Weights(0, first)
        x_rings = [None, None]
        attended_low[0], turned[0], stats[0] = run_attention(0, g_steps)
        hidden[0], moe_in[0], probs[0], message = run_route(0, attended_low[0])
        g_steps = [ring.step() for ring in g_rings]
        x_rings[0] = Ring(message)
        attended_low[1], turned[1], stats[1] = run_attention(1, early.hand_on() + (message,))
        late = Weights(1, message)
        hidden[1], moe_in[1], probs[1], message = run_route(1, attended_low[1], g_steps)
        x_rings[1] = Ring(message)
        x_rings[0].step()
        x_rings[0].step()
        x_rings[1].step()
        early_full = early.full()
        got = {}
        got[0, 0] = one_experts(0, 0, early_full, late.hand_on() + (x_rings[1].step(),))
        late_full = late.full()
        got[1, 0] = one_experts(1, 0, late_full, (got[0, 0][4], x_rings[1].step()))

        def run_combine(m, kind, after):
            pieces = [got[c, m][4:] for c in range(2)]
            senses = [p[2] for p in pieces] if kind else None
            sources = [p[kind] for p in pieces]
            mine, *others = combine(index, g_rings[m].runs(), sources, senses, after)
            return mine, others

        mine, others = run_combine(0, 1, (got[1, 0][4],))
        in_home = [Home(mine, others)]
        got[0, 1] = one_experts(0, 1, early_full, (in_home[0].total,))
        got[1, 1] = one_experts(1, 1, late_full, (got[0, 1][4], in_home[0].step()))
        mine, others = run_combine(1, 1, (got[1, 1][4], in_home[0].step()))
        in_home.append(Home(mine, others))
        in_home[0].end()
        grads = [expert_grads([got[0, m][:4] for m in micros], (in_home[1].total,))]
        reducing = [[reduce_first(p) for p in grads[0]]]
        grads.append(
            expert_grads([got[1, m][:4] for m in micros], (grads[0][0][0], in_home[0].total))
        )
        reducing.append([reduce_first(p) for p in grads[1]])
        step_one = in_home[1].step()
        hidden_grad, branch, attended_grad, logit, norm_two_0 = run_hidden_back(
            0, in_home[0].total, (grads[1][0][0], step_one)
        )
        hidden_grads, branches, logits = [hidden_grad], [branch], [logit]
        query_grad, *parts = run_attend_back(0, attended_grad, (in_home[1].step(),))
        query_grads, kv_parts = [query_grad], [parts]

        def send_back(parts):
            far = lax.ppermute(parts[3], "ctx", [(2, 3), (3, 2)])
            return add(parts[2], far).astype(BF)

        def arrive_back(parts, along):
            near = lax.ppermute(parts[1], "ctx", [(1, 0), (3, 2)])
            return [parts[0], near, lax.ppermute(along, "ctx", [(2, 0), (3, 1)])]

        mine, others = run_combine(0, 0, (query_grad,))
        out_home = [Home(mine, others)]
        along = [send_back(parts)]
        first_adds = [a for r in reducing[0] for a in r[3:]]
        hidden_grad, branch, attended_grad, logit, norm_two_1 = run_hidden_back(
            1, in_home[1].end(), (mine, along[0], *first_adds)
        )
        hidden_grads.append(hidden_grad)
        branches.append(branch)
        logits.append(logit)
        query_grad, *parts = run_attend_back(1, attended_grad, (out_home[0].total,))
        query_grads.append(query_grad)
        kv_parts.append(parts)
        along.append(send_back(parts))
        mine, others = run_combine(1, 0, (query_grad, out_home[0].step()))
        out_home.append(Home(mine, others))
        backs[0] = run_input_back(
            0, query_grads[0], arrive_back(kv_parts[0], along[0]), hidden_grads[0], (mine, along[1])
        )
        second_adds = [a for r in reducing[1] for a in r[3:]]
        backs[1] = run_input_back(
            1,
            query_grads[1],
            arrive_back(kv_parts[1], along[1]),
            hidden_grads[1],
            (backs[0][1], out_home[1].total, out_home[0].step(), *second_adds),
        )
        norm_two_sum = norm_two_0 + norm_two_1
        for m in micros:
            outputs[m] = finish_output(m, out_home[m].end())
        gate_up_sum, down_sum = [
            swap_out(jnp.concatenate([reduce_last(r[i]) for r in reducing], 0), 1 + i)
            for i in range(2)
        ]
    else:
        full = [gather_chips(later(a, first)) for a in (gate_up_own, down_own)]
        normed_in, query, *kv_own = project(tokens, first, gain_one, cosine_w, sine_w)
        kv_blocks, last = [None] * micro_count, first
        branches, logits = [None] * micro_count, [None] * micro_count
        norm_two_sum, gate_up_grad, down_grad = 0.0, 0.0, 0.0
        group = min(exp_count, 4)
        for m in micros:
            kv_blocks[m] = gather_ctx(later(kv_own[m], last))
            attended_low[m], turned[m], stats[m] = run_attention(m)
            hidden[m], moe_in[m], probs[m], message = run_route(m, attended_low[m])
            x_runs, g_runs = Ring(message).runs(), g_rings[m].runs()
            mines, others = [[], []], [[], []]
            for g in range(0, exp_count, group):
                span = slice(2 * g, 2 * (g + group))
                after = (last,)
                *kept, out, back, sens = experts(
                    index, 0, x_runs[span], g_runs[span], *full, after=after
                )
                gate_up_grad += jnp.einsum(
                    "esd,esf->edf", kept[0], kept[2], preferred_element_type=F32
                )
                down_grad += jnp.einsum("esf,esd->efd", kept[3], kept[1], preferred_element_type=F32)
                for i, source in enumerate((out, back)):
                    mine, *other = combine(
                        index, g_runs[span], [source], [sens] if i else None, after
                    )
                    mines[i] += [mine[k] for k in range(group)]
                    others[i] += other
                last = mine
            in_total = Home(mines[1], others[1]).end()
            outputs[m] = finish_output(m, Home(mines[0], others[0]).end())
            last = outputs[m]
            hidden_grad, branches[m], attended_grad, logits[m], norm = run_hidden_back(m, in_total)
            norm_two_sum += norm
            query_grad, *parts = run_attend_back(m, attended_grad)
            kv_sum = reduce_ctx(parts).astype(BF)
            backs[m] = run_input_back(m, query_grad, [kv_sum], hidden_grad)
        gate_up_sum = jnp.split(gate_up_grad.astype(BF), chips, 1)
        down_sum = jnp.split(down_grad.astype(BF), chips, 2)
        gate_up_sum = swap_out(reduce_chips(gate_up_sum), 1)
        down_sum = swap_out(reduce_chips(down_sum), 2)

    input_grads = [b[0] for b in backs]
    lows = [b[1] for b in backs]
    norm_one_sum = sum(b[2] for b in backs)

    def stack_rows(parts):
        return jnp.concatenate(parts, 0)

    attended_rows = stack_rows(attended_low)
    moe_rows = stack_rows(moe_in)
    second_sum = dot_tn(attended_rows, stack_rows(branches)).astype(BF)
    router_sum = dot_tn(moe_rows, stack_rows(logits))[:, :EXPERTS]
    first_sum = dot_tn(normed_in, stack_rows(lows)).astype(BF)
    small = jnp.concatenate([norm_one_sum.T, norm_two_sum.T, router_sum], 1).astype(BF)
    small = jnp.pad(small, ((0, 0), (0, 128 - small.shape[1])))
    packed = jnp.concatenate([first_sum, second_sum, small], 1)
    total = lax.psum_scatter(packed, PLANE, scatter_dimension=0, tiled=True)
    total = lax.psum(total, "exp").astype(F32)
    cuts = [H * HD, (H + KVH) * HD, (H + 2 * KVH) * HD, (H + 2 * KVH) * HD + width]
    query_grad, key_grad, value_grad, out_grad, small = jnp.split(total, cuts, 1)
    return (
        jnp.stack(outputs)[:, None],
        jnp.stack(input_grads)[:, None],
        small[:, 0],
        small[:, 1],
        query_grad,
        key_grad,
        value_grad,
        out_grad,
        small[:, 2 : 2 + EXPERTS],
        gate_up_sum[..., :FF],
        gate_up_sum[..., FF:],
        down_sum,
    )


def solution(mesh):
    rows = P(None, ("dp", "exp"), "ctx", None)
    row_shard = P(PLANE, None)
    return jax.shard_map(
        on_device,
        mesh=mesh,
        in_specs=(
            rows,
            rows,
            rows,
            P(PLANE),
            P(PLANE),
            row_shard,
            row_shard,
            row_shard,
            row_shard,
            row_shard,
            P("exp", PLANE, None),
            P("exp", PLANE, None),
            P("exp", None, PLANE),
        ),
        out_specs=(
            rows,
            rows,
            P(PLANE),
            P(PLANE),
            row_shard,
            row_shard,
            row_shard,
            row_shard,
            row_shard,
            P("exp", PLANE, None),
            P("exp", PLANE, None),
            P("exp", None, PLANE),
        ),
        check_vma=False,
    )
```

```python
import jax
import jax.numpy as jnp
from jax import lax
from jax.experimental import pallas as pl
from jax.experimental.pallas import tpu as pltpu
from jax.sharding import PartitionSpec as P

H = 16
KVH = 8
HD = 64
EXPERTS = 32
FF = 512
TOPK = 8
BLOCK = 256
CAP = 72
PAD = 80
GROUP = H // KVH

EPSILON = 1e-06
BASE_THETA = 10000.0
NEGATIVE = -1e30
ATTENTION_MULT = 0.015625
RESIDUAL_MULT = 0.22

PLANE = ("dp", "ctx")
BF = jnp.bfloat16
F32 = jnp.float32


def dot(left, right):
    return jnp.dot(left, right, preferred_element_type=F32)


def dot_tn(left, right):
    return lax.dot_general(left, right, (((0,), (0,)), ((), ())), preferred_element_type=F32)


def dot_nt(left, right):
    return lax.dot_general(left, right, (((1,), (1,)), ((), ())), preferred_element_type=F32)


def add(left, right):
    return left.astype(F32) + right.astype(F32)


def relative(blocks, index):
    count = len(blocks)
    bit = 1
    while bit < count:
        on = (index & bit) != 0
        blocks = [jnp.where(on, blocks[j ^ bit], blocks[j]) for j in range(count)]
        bit *= 2
    return blocks


def reorder(array, count, index, axis):
    return jnp.concatenate(relative(jnp.split(array, count, axis), index), axis)


def plane_swap(array, mask):
    count = lax.axis_size("dp") * lax.axis_size("ctx")
    return lax.ppermute(array, PLANE, [(i, i ^ mask) for i in range(count)])


def sibling(array):
    return plane_swap(array, 1)


def halves(array):
    return jnp.split(array, 2, -2)


def gather_chips(own):
    chips = lax.axis_size("dp") * lax.axis_size("ctx") // 2
    if chips == 4:
        along_x, along_y = plane_swap(own, 2), plane_swap(own, 4)
        first, last = halves(along_x)[0], halves(along_y)[1]
        far = jnp.concatenate([plane_swap(first, 4), plane_swap(last, 2)], -2)
        return [own, along_x, along_y, far]
    blocks, mask = [own], 1
    while mask < chips:
        blocks = blocks + [plane_swap(b, 2 * mask) for b in blocks]
        mask *= 2
    return blocks


def gather_plane(own):
    blocks = []
    for block in gather_chips(own):
        blocks += [block, sibling(block)]
    return blocks


def reduce_chips(blocks):
    chips = len(blocks)
    if chips == 4:
        upper, lower = zip(*[halves(b) for b in blocks])
        from_x = plane_swap(jnp.concatenate([upper[1], upper[3]], -2), 2)
        from_y = plane_swap(jnp.concatenate([lower[2], lower[3]], -2), 4)
        x_own, x_rest = halves(from_x)
        y_own, y_rest = halves(from_y)
        upper_last = plane_swap(add(upper[2], x_rest).astype(BF), 4)
        lower_last = plane_swap(add(lower[1], y_rest).astype(BF), 2)
        top = add(upper[0], x_own) + upper_last.astype(F32)
        low = add(lower[0], y_own) + lower_last.astype(F32)
        return jnp.concatenate([top, low], -2)
    mask = chips // 2
    while mask:
        blocks = [
            add(blocks[j], plane_swap(blocks[j + mask], 2 * mask)).astype(BF) for j in range(mask)
        ]
        mask //= 2
    return blocks[0].astype(F32)


def reduce_plane(blocks):
    other = sibling(jnp.concatenate(blocks[1::2], -2))
    others = jnp.split(other, len(blocks) // 2, -2)
    return reduce_chips([add(a, b).astype(BF) for a, b in zip(blocks[0::2], others)])


def gather_ctx(own):
    count = lax.axis_size("ctx")
    if count == 4:
        near = lax.ppermute(own, "ctx", [(0, 1), (2, 3)])
        along = lax.ppermute(own, "ctx", [(0, 2), (1, 3)])
        far = lax.ppermute(along, "ctx", [(2, 3), (3, 2)])
        return [own, near, along, far]
    blocks, mask = [own], 1
    while mask < count:
        blocks = blocks + [
            lax.ppermute(b, "ctx", [(i, i ^ mask) for i in range(count)]) for b in blocks
        ]
        mask *= 2
    return blocks


def reduce_ctx(blocks):
    count = lax.axis_size("ctx")
    if count == 4:
        far = lax.ppermute(blocks[3], "ctx", [(2, 3), (3, 2)])
        along = lax.ppermute(add(blocks[2], far).astype(BF), "ctx", [(2, 0), (3, 1)])
        near = lax.ppermute(blocks[1], "ctx", [(1, 0), (3, 2)])
        return add(blocks[0], near) + along.astype(F32)
    mask = count // 2
    while mask:
        perm = [(i, i ^ mask) for i in range(count)]
        blocks = [
            add(blocks[j], lax.ppermute(blocks[j + mask], "ctx", perm)).astype(BF)
            for j in range(mask)
        ]
        mask //= 2
    return blocks[0].astype(F32)


def ring_step(array):
    count = lax.axis_size("exp")
    return lax.ppermute(array, "exp", [(i, (i + 1) % count) for i in range(count)])


def gather_ring(own):
    blocks = [own]
    for _ in range(lax.axis_size("exp") - 1):
        blocks.append(ring_step(blocks[-1]))
    return blocks


def reduce_ring(blocks):
    count = len(blocks)
    total = blocks[1 % count]
    for k in range(2, count + 1):
        total = add(ring_step(total), blocks[k % count]).astype(BF)
    return total


def rotation(offset, row_count):
    half_size = HD // 2
    inverse = jnp.exp(jnp.arange(half_size, dtype=F32) * (-2.0 * jnp.log(F32(BASE_THETA)) / HD))
    places = (offset + jnp.arange(row_count, dtype=jnp.int32)).astype(F32)
    angles = places[:, None] * inverse[None, :]
    return (jnp.cos(angles), jnp.sin(angles))


def rope(pair, cosine, sine):
    lane = lax.broadcasted_iota(jnp.int32, pair.shape, 1)
    former = lane % HD < HD // 2
    turned = jnp.where(
        former, pltpu.roll(pair, 2 * HD - HD // 2, 1), pltpu.roll(pair, HD // 2, 1)
    )
    return pair * cosine + turned * sine


def inverse_rms(values):
    return lax.rsqrt(jnp.mean(values * values, -1, keepdims=True) + EPSILON)


def spec(shape, index=None):
    index = index or (lambda *_: (0,) * len(shape))
    return pl.BlockSpec(shape, index)


def once(shape, index=None):
    index = index or (lambda *_: (0,) * len(shape))
    return pl.BlockSpec(shape, index, pipeline_mode=pl.Buffered(1))


def shape_of(shape, kind):
    return jax.ShapeDtypeStruct(shape, kind)


COST = {
    "prepare": 4, "pack": 4, "merge": 3, "project": 10, "attend": 17, "attend_back": 20, "route": 5, "experts": 18,
    "expert_grads": 14, "combine": 6, "carry_on": 4, "finish": 5, "fold": 3, "unpack": 8, "hidden_back": 6,
    "input_back": 6, "dense_grads": 9, "total_of": 5,
}


def call(
    body, grid, in_specs, out_specs, out_shape, scratch, args, flops, moved, limit=56, after=()
):
    count, first = len(after), len(args)

    def ordered(*refs):
        body(*refs[:first], *refs[first + count :])

    return pl.pallas_call(
        ordered,
        grid_spec=pltpu.PrefetchScalarGridSpec(
            num_scalar_prefetch=1,
            grid=grid,
            in_specs=list(in_specs) + [pl.BlockSpec(memory_space=pl.ANY)] * count,
            out_specs=out_specs,
            scratch_shapes=scratch,
        ),
        out_shape=out_shape,
        compiler_params=pltpu.CompilerParams(vmem_limit_bytes=limit << 20),
        cost_estimate=pl.CostEstimate(
            flops=int(COST[body.__qualname__.split(".")[0]] * 5.768e+09), bytes_accessed=1024, transcendentals=0
        ),
    )(*args, *after)


def lanes(index, size):
    return pl.ds(pl.multiple_of(index * size, size), size)


def shards_of(pieces, rows):
    found, j = [], 0
    for piece in pieces:
        if piece.shape[0] == rows:
            found.append((j, 0))
            j += 1
        else:
            found.append((j, 0) if not found or found[-1][0] != j else (j, rows // 2))
            j += found[-1][1] > 0
    return found


def fill(scratch, refs, base, rows):
    for ref, (j, row) in zip(refs, shards_of(refs, rows)):
        count = ref.shape[0]
        at = pl.multiple_of((j ^ base) * rows + row, count)
        scratch[pl.ds(at, count), :] = ref[...]


def prepare(index, routes, cotangent, chips):
    micro, rows, width = cotangent.shape
    part = width // chips

    def body(index_ref, routes_ref, cotangent_ref, picks_ref, message_ref):
        chip = index_ref[0]
        earlier = lax.broadcasted_iota(jnp.int32, (rows, rows), 0) > lax.broadcasted_iota(
            jnp.int32, (rows, rows), 1
        )
        earlier = jnp.where(earlier, 1.0, 0.0).astype(BF)
        expert = lax.broadcasted_iota(jnp.int32, (rows, 128), 1)
        for m in range(micro):
            chosen = routes_ref[m]
            pick = jnp.zeros((rows, 128), F32)
            for k in range(TOPK):
                pick = pick + jnp.where(chosen[:, k : k + 1] == expert, 1.0, 0.0)
            rank = dot(earlier, pick.astype(BF))
            slot = jnp.where((pick > 0.0) & (rank < CAP), rank, -1.0).T
            picks_ref[m] = pick
            out = message_ref.at[m]
            for j in range(chips):
                out[:rows, j * part : (j + 1) * part] = cotangent_ref[m, :, lanes(j ^ chip, part)]
            out[rows:, :] = jnp.concatenate(
                [slot[:16], slot[16:32], jnp.zeros((16, width - 2 * rows), F32)], 1
            ).astype(BF)

    message = (micro, rows + 16, width)
    return call(
        body,
        (1,),
        [spec(routes.shape), spec(cotangent.shape)],
        [spec((micro, rows, 128)), spec(message)],
        [shape_of((micro, rows, 128), F32), shape_of(message, BF)],
        [],
        (index, routes, cotangent),
        1 << 26,
        4 << 20,
    )


def project(index, tokens, pieces, cosine, sine, after=()):
    micro, rows, width = tokens.shape
    shard = pieces[0].shape[0]
    columns = pieces[0].shape[1]
    queries, keys = H * HD, KVH * HD
    inner = queries + 2 * keys + 128
    count = len(pieces)

    def body(index_ref, tokens_ref, cosine_ref, sine_ref, *refs):
        weight, second_ref, gains_ref, query_ref, *rest = refs[count:]
        normed_refs, kv_refs = rest[:micro], rest[micro : 2 * micro]
        fill(weight, [r.at[:, :inner] for r in refs[:count]], index_ref[5], shard)
        fill(second_ref, [r.at[:, inner:] for r in refs[:count]], index_ref[5], shard)
        gains_ref[...] = weight[:, inner - 128 :].astype(F32).T[:8]
        gain = gains_ref[:1, :]
        cos, sin = cosine_ref[...], sine_ref[...]
        for m in range(micro):
            values = tokens_ref[m].astype(F32)
            normed = (values * inverse_rms(values) * gain).astype(BF)
            normed_refs[m][...] = normed
            for j in range(queries // 256):
                got = dot(normed, weight[:, j * 256 : (j + 1) * 256])
                for i in range(2):
                    turned = rope(got[:, i * 128 : (i + 1) * 128], cos, sin)
                    at = j * 256 + i * 128
                    query_ref[m, :, at : at + 128] = turned.astype(BF)
            for j in range(keys // 256):
                got = dot(normed, weight[:, queries + j * 256 : queries + (j + 1) * 256])
                for i in range(2):
                    turned = rope(got[:, i * 128 : (i + 1) * 128], cos, sin)
                    at = j * 256 + i * 128
                    kv_refs[m][:, at : at + 128] = turned.astype(BF)
            got = dot(normed, weight[:, queries + keys : queries + 2 * keys])
            kv_refs[m][:, keys:] = got.astype(BF)

    shapes = [((width, inner), BF), ((width, columns - inner), BF), ((8, width), F32)]
    shapes += [((micro, rows, queries), BF)]
    shapes += [((rows, width), BF)] * micro + [((rows, 2 * keys), BF)] * micro
    return call(
        body,
        (1,),
        [spec(a.shape) for a in (tokens, cosine, sine, *pieces)],
        [spec(n) for n, _ in shapes],
        [shape_of(n, kind) for n, kind in shapes],
        [],
        (index, tokens, cosine, sine, *pieces),
        2 * micro * rows * width * columns,
        12 << 20,
        after=after,
    )


def place_heads(pair, which):
    lane = lax.broadcasted_iota(jnp.int32, pair.shape, 1)
    mine = (lane < HD) if which == 0 else (lane >= HD)
    moved = pltpu.roll(pair, HD, 1)
    both = (pair, moved) if which == 0 else (moved, pair)
    return jnp.concatenate([jnp.where(mine, b, 0.0) for b in both], 0)


def attend(index, query, blocks, after=()):
    rows = query.shape[0]
    count = len(blocks)
    steps = KVH // 2
    width = H * HD

    def body(index_ref, query_ref, *refs):
        key_refs, value_refs = refs[:count], refs[count : 2 * count]
        low_ref, turned_ref, stat_ref = refs[2 * count : 2 * count + 3]
        top, total, mixed = refs[2 * count + 3 :]
        ctx = index_ref[2]
        heads = []
        for a in range(2):
            pair = query_ref[:, a * 128 : (a + 1) * 128].astype(F32) * ATTENTION_MULT
            heads.append(place_heads(pair, a).T.astype(BF))

        def visit(j):
            key, value = key_refs[j][...], value_refs[j][...]
            for a in range(2):
                scores = dot(key, heads[a])
                peak = jnp.max(scores, 0, keepdims=True)
                if j:
                    peak = jnp.maximum(peak, top[a])
                expo = jnp.exp(scores - peak)
                added = jnp.sum(expo, 0, keepdims=True)
                got = dot_tn(value, expo.astype(BF))[a * HD : (a + 1) * HD]
                if j:
                    scale = jnp.exp(top[a] - peak)
                    added = added + total[a] * scale
                    got = got + mixed[a] * scale
                top[a] = peak
                total[a] = added
                mixed[a] = got

        visit(0)
        for j in range(1, count):
            pl.when((ctx ^ j) <= ctx)(lambda j=j: visit(j))
        for a in range(2):
            got = mixed[a] / total[a]
            turned = jnp.concatenate([got[:, :rows], got[:, rows:]], 0)
            turned_ref[a * 128 : (a + 1) * 128, :] = turned
            low_ref[:, a * 128 : (a + 1) * 128] = turned.T.astype(BF)
            stat_ref[0, a : a + 1, :] = top[a] + jnp.log(total[a])

    keys = [spec((rows, 128), lambda i, *_: (0, i))] * count
    values = [spec((rows, 128), lambda i, *_: (0, i + steps))] * count
    return call(
        body,
        (steps,),
        [spec((rows, 256), lambda i, *_: (0, i))] + keys + values,
        [
            spec((rows, 256), lambda i, *_: (0, i)),
            spec((256, rows), lambda i, *_: (i, 0)),
            spec((1, 2, 2 * rows), lambda i, *_: (i, 0, 0)),
        ],
        [
            shape_of((rows, width), BF),
            shape_of((width, rows), F32),
            shape_of((steps, 2, 2 * rows), F32),
        ],
        [
            pltpu.VMEM((2, 1, 2 * rows), F32),
            pltpu.VMEM((2, 1, 2 * rows), F32),
            pltpu.VMEM((2, HD, 2 * rows), F32),
        ],
        (index, query, *blocks, *blocks),
        8 * rows * rows * count * width,
        6 << 20,
        after=after,
    )


def attend_back(index, query, blocks, attended_grad, attended, stats, cosine, sine, after=()):
    rows = query.shape[0]
    count = len(blocks)
    steps = KVH // 2
    half = HD // 2

    def body(index_ref, query_ref, grad_ref, attended_ref, stat_ref, cosine_ref, sine_ref, *refs):
        key_refs, value_refs = refs[:count], refs[count : 2 * count]
        query_out, kv_out = refs[2 * count], refs[2 * count + 1 : 3 * count + 1]
        (query_sum,) = refs[3 * count + 1 :]
        ctx = index_ref[2]
        step = pl.program_id(0)
        heads, grads, heads_t, grads_t, deltas = [], [], [], [], []
        for a in range(2):
            at = slice(a * 128, (a + 1) * 128)
            placed = place_heads(query_ref[:, at].astype(F32) * ATTENTION_MULT, a)
            heads.append(placed.astype(BF))
            heads_t.append(placed.T.astype(BF))
            pair = grad_ref[:, at].astype(F32)
            placed = place_heads(pair, a)
            grads.append(placed.astype(BF))
            grads_t.append(placed.T.astype(BF))
            product = pair.T * attended_ref[at, :]
            deltas.append(
                jnp.concatenate(
                    [jnp.sum(product[i * HD : (i + 1) * HD], 0, keepdims=True) for i in range(2)], 1
                )
            )

        def visit(j):
            key, value = key_refs[j][...], value_refs[j][...]
            key_sum, value_sum = 0.0, 0.0
            for a in range(2):
                probs = jnp.exp(dot(key, heads_t[a]) - stat_ref[0, a : a + 1, :])
                score_grad = (probs * (dot(value, grads_t[a]) - deltas[a])).astype(BF)
                key_sum = key_sum + dot(score_grad, heads[a])
                value_sum = value_sum + dot(probs.astype(BF), grads[a])
                got = dot_tn(key, score_grad)[a * HD : (a + 1) * HD]
                if j:
                    got = got + query_sum[a]
                query_sum[a] = got
            kv_out[j][:, lanes(step, 128)] = key_sum.astype(BF)
            kv_out[j][:, lanes(step + steps, 128)] = value_sum.astype(BF)

        visit(0)
        for j in range(1, count):
            reach = (ctx ^ j) <= ctx
            pl.when(reach)(lambda j=j: visit(j))

            @pl.when(jnp.logical_not(reach) & (step == 0))
            def _(j=j):
                kv_out[j][...] = jnp.zeros_like(kv_out[j])

        cos, sin = cosine_ref[...], sine_ref[...]
        for a in range(2):
            got = query_sum[a] * ATTENTION_MULT
            pieces = []
            for i in range(2):
                former = got[:half, i * rows : (i + 1) * rows]
                latter = got[half:, i * rows : (i + 1) * rows]
                pieces += [former * cos + latter * sin, latter * cos - former * sin]
            query_out[:, a * 128 : (a + 1) * 128] = jnp.concatenate(pieces, 0).T.astype(BF)

    wide = spec((rows, 256), lambda i, *_: (0, i))
    keys = [spec((rows, 128), lambda i, *_: (0, i))] * count
    values = [spec((rows, 128), lambda i, *_: (0, i + steps))] * count
    kv = (rows, 2 * KVH * HD)
    return call(
        body,
        (steps,),
        [
            wide,
            wide,
            spec((256, rows), lambda i, *_: (i, 0)),
            spec((1, 2, 2 * rows), lambda i, *_: (i, 0, 0)),
            spec(cosine.shape),
            spec(sine.shape),
        ]
        + keys
        + values,
        [wide] + [spec(kv)] * count,
        [shape_of((rows, H * HD), BF)] + [shape_of(kv, BF)] * count,
        [pltpu.VMEM((2, HD, 2 * rows), F32)],
        (index, query, attended_grad, attended, stats, cosine, sine, *blocks, *blocks),
        20 * rows * rows * count * H * HD,
        8 << 20,
        after=after,
    )


def route(index, attended, tokens, second, gains, picks, chips, copies, after=()):
    rows, width = attended.shape
    part = width // chips

    def body(
        index_ref, attended_ref, tokens_ref, second_ref, gains_ref, picks_ref,
        hidden_ref, moe_ref, probs_ref, message_ref,
    ):
        chip = index_ref[0]
        hidden = tokens_ref[...].astype(F32) + RESIDUAL_MULT * dot(
            attended_ref[...], second_ref[:, :width]
        )
        hidden_ref[...] = hidden
        moe_in = (hidden * inverse_rms(hidden) * gains_ref[1:2, :]).astype(BF)
        moe_ref[...] = moe_in
        picked = picks_ref[...] > 0.0
        chosen = jnp.where(picked, dot(moe_in, second_ref[:, width:]), NEGATIVE)
        expo = jnp.where(picked, jnp.exp(chosen - jnp.max(chosen, -1, keepdims=True)), 0.0)
        probs = expo / jnp.sum(expo, -1, keepdims=True)
        probs_ref[...] = probs
        turned = probs.T
        high = turned.astype(BF).astype(F32)
        low = turned - high
        tail = jnp.concatenate([high[:16], high[16:32], low[:16], low[16:32]], 1).astype(BF)
        for i in range(copies):
            for j in range(chips):
                message_ref[i, :rows, j * part : (j + 1) * part] = moe_ref[:, lanes(j ^ chip, part)]
            message_ref[i, rows:, :] = tail

    args = (index, attended, tokens, second, gains, picks)
    shapes = [((rows, width), F32), ((rows, width), BF), ((rows, 128), F32)]
    shapes += [((copies, rows + 16, width), BF)]
    return call(
        body,
        (1,),
        [spec(a.shape) for a in args[1:]],
        [spec(n) for n, _ in shapes],
        [shape_of(n, kind) for n, kind in shapes],
        [],
        args,
        2 * rows * width * width,
        6 << 20,
        after=after,
    )


def pack(index, other, w_gate, w_up, w_down, after=()):
    count, shard = w_gate.shape[0] // 2, w_gate.shape[1]
    deep_rows = FF // 8

    def body(index_ref, gate_ref, up_ref, down_ref, out_ref):
        out_ref[0, :shard, :FF] = gate_ref[0]
        out_ref[0, :shard, FF:] = up_ref[0]
        for q in range(8):
            out_ref[0, shard:, q * shard : (q + 1) * shard] = down_ref[
                0, q * deep_rows : (q + 1) * deep_rows, :
            ]

    def take(i, index):
        core = 1 - index[1] if other else index[1]
        return (core * count + i, 0, 0)

    size = (shard + deep_rows, 2 * FF)
    return call(
        body,
        (count,),
        [spec((1,) + a.shape[1:], take) for a in (w_gate, w_up, w_down)],
        spec((1,) + size, lambda i, *_: (i, 0, 0)),
        shape_of((count,) + size, BF),
        [],
        (index, w_gate, w_up, w_down),
        1024,
        1024,
        after=after,
    )


def merge(index, first, count, mine, got, after=()):
    rows, width = mine.shape[1:]

    def body(index_ref, mine_ref, got_ref, out_ref):
        core = index_ref[1]
        out_ref[0, pl.ds(pl.multiple_of(core * rows, rows), rows), :] = mine_ref[0]
        out_ref[0, pl.ds(pl.multiple_of((1 - core) * rows, rows), rows), :] = got_ref[0]

    some = spec((1, rows, width), lambda i, *_: (first + i, 0, 0))
    return call(
        body,
        (count,),
        [some, some],
        spec((1, 2 * rows, width), lambda i, *_: (i, 0, 0)),
        shape_of((count, 2 * rows, width), BF),
        [],
        (index, mine, got),
        1024,
        1024,
        after=after,
    )


def total_of(index, left, right, after=()):
    def body(index_ref, left_ref, right_ref, out_ref):
        out_ref[...] = add(left_ref[...], right_ref[...]).astype(BF)

    some = spec((1,) + left.shape[1:], lambda i, *_: (i, 0, 0))
    return call(
        body,
        (left.shape[0],),
        [some, some],
        some,
        shape_of(left.shape, BF),
        [],
        (index, left, right),
        1024,
        1024,
        after=after,
    )


def expert_row(ref, start, rows, expert, first):
    table = ref[start : start + 16, pl.ds(pl.multiple_of((expert // 16) * rows + first, rows), rows)]
    table = table.astype(F32)
    line = lax.broadcasted_iota(jnp.int32, table.shape, 0) == expert % 16
    return jnp.sum(jnp.where(line, table, 0.0), 0, keepdims=True)


def slots_of(row, count=CAP):
    slot = lax.broadcasted_iota(jnp.int32, (count, row.shape[1]), 0).astype(F32)
    return jnp.where(slot == row, 1.0, 0.0)


def run_specs(shape, micro, runs, first, count):
    if len(shape) == 3:
        return [once((1, count, shape[2]), lambda *_, k=k: (k, first, 0)) for k in runs for _ in range(2)]
    return [
        once((1, 1, count, shape[3]), lambda *_, k=k: (k, micro, first, 0))
        for k in runs
        for _ in range(2)
    ]


def experts(index, offset, token_pair, grad_pair, micro, runs, weights, after=()):
    count = weights[0].shape[0]
    total = 2 * len(runs)
    rows, width = token_pair[0].shape[1] - 16, token_pair[0].shape[2]
    slots, padded = total * CAP, total * PAD
    pieces = len(weights)
    packed = pieces == 5
    shard, deep_rows, part = width // 8, FF // 8, width // 8

    def body(index_ref, *refs):
        tokens_in = [r.at[0] for r in refs[:total]]
        grads_in = [r.at[0, 0] for r in refs[total : 2 * total]]
        at = 2 * total
        weights_in = refs[at : at + pieces]
        at += pieces
        received_ref, pair_ref, inner_ref, hidden_ref, out_ref, back_ref, sens_ref = refs[at : at + 7]
        received, grads, probs_at, *whole = refs[at + 7 :]
        step = pl.program_id(0)

        @pl.when(step == 0)
        def _():
            for k in range(0, total, 2):
                found = []
                for r in (k, k + 1):
                    takes, probs = [], []
                    for i in range(count):
                        expert = index_ref[3] + offset + i
                        take = slots_of(expert_row(grads_in[r], rows, rows, expert, 0))
                        prob = expert_row(tokens_in[r], rows, rows, expert, 0) + expert_row(
                            tokens_in[r], rows, rows, expert, 2 * rows
                        )
                        takes.append(take)
                        probs.append(jnp.sum(take * prob, 1, keepdims=True))
                    take = jnp.concatenate(takes, 0).astype(BF)
                    found.append(
                        (dot(take, tokens_in[r][:rows, :]), dot(take, grads_in[r][:rows, :]), probs)
                    )
                for i in range(count):
                    span = slice(k * CAP, (k + 2) * CAP)
                    pick = slice(i * CAP, (i + 1) * CAP)
                    received[i, span, :] = jnp.concatenate([f[0][pick] for f in found], 0).astype(BF)
                    grads[i, span, :] = jnp.concatenate([f[1][pick] for f in found], 0).astype(BF)
                    prob = jnp.concatenate([f[2][i] for f in found], 0)
                    probs_at[i, span, :] = jnp.broadcast_to(prob, (2 * CAP, 128))

        if packed:
            wide, deep = whole
            own, along_x, along_y, *far = [r.at[0] for r in weights_in]
            size = shard + deep_rows
            for c in range(8):
                if c < 6:
                    source = (own, along_x, along_y)[c // 2].at[(c % 2) * size : (c % 2 + 1) * size]
                else:
                    source = far[c - 6]
                wide[c * shard : (c + 1) * shard, :] = source[:shard, :]
                for q in range(8):
                    deep[q * deep_rows : (q + 1) * deep_rows, c * part : (c + 1) * part] = source[
                        shard:, q * part : (q + 1) * part
                    ]
        else:
            wide, deep = [r.at[0] for r in weights_in]

        rows_in = received[step]
        received_ref[0] = rows_in
        prob = probs_at[step][:, :1]
        scaled = RESIDUAL_MULT * grads[step].astype(F32)
        pair = (prob * scaled).astype(BF)
        pair_ref[0] = pair
        both = dot(rows_in, wide[...])
        gate_h, up_h = both[:, :FF], both[:, FF:]
        sigma = jax.nn.sigmoid(gate_h)
        silu_gate = gate_h * sigma
        hidden = (silu_gate * up_h).astype(BF)
        hidden_ref[0] = hidden
        inner = dot_nt(pair, deep[...])
        gate_d = (inner * up_h * sigma * (1.0 + gate_h * (1.0 - sigma))).astype(BF)
        up_d = (inner * silu_gate).astype(BF)
        inner_ref[0, :, :FF] = gate_d
        inner_ref[0, :, FF:] = up_d
        out = dot(hidden, deep[...]).astype(BF).astype(F32)

        def put(ref, value):
            blank = jnp.zeros((PAD - CAP, width), F32)
            for r in range(total):
                run = jnp.concatenate([value[r * CAP : (r + 1) * CAP], blank], 0)
                ref[0, r * PAD : (r + 1) * PAD, :] = run.astype(BF)

        put(out_ref, prob * out)
        sens = jnp.sum(out * scaled, 1, keepdims=True)
        expert = index_ref[3] + offset + step
        for r in range(total):
            take = slots_of(expert_row(grads_in[r], rows, rows, expert, 0))
            sens_ref[0, r // 2, r % 2 : r % 2 + 1, :] = jnp.sum(
                take * sens[r * CAP : (r + 1) * CAP], 0, keepdims=True
            )
        put(back_ref, dot_nt(inner_ref[0], wide[...]))

    step = lambda i, *_: (i, 0, 0)
    sizes = [(slots, n) for n in (width, width, 2 * FF, FF)] + [(padded, width)] * 2
    run_in = [
        n for pair in (token_pair, grad_pair) for n in run_specs(pair[0].shape, micro, runs, 0, rows + 16)
    ]
    return call(
        body,
        (count,),
        run_in + [spec((1,) + a.shape[1:], step) for a in weights],
        [spec((1,) + n, step) for n in sizes]
        + [spec((1, total // 2, 2, rows), lambda i, *_: (i, 0, 0, 0))],
        [shape_of((count,) + n, BF) for n in sizes]
        + [shape_of((count, total // 2, 2, rows), F32)],
        [
            pltpu.VMEM((count, slots, width), BF),
            pltpu.VMEM((count, slots, width), BF),
            pltpu.VMEM((count, slots, 128), F32),
        ]
        + ([pltpu.VMEM((width, 2 * FF), BF), pltpu.VMEM((FF, width), BF)] if packed else []),
        (index, *(list(token_pair) * len(runs)), *(list(grad_pair) * len(runs)), *weights),
        count * slots * width * FF * 16,
        count * slots * 14 << 10,
        60,
        after,
    )


def expert_grads(index, parts, after=()):
    count, slots, width = parts[0][0].shape
    shard, deep_rows, part = width // 8, FF // 8, width // 8
    size = shard + deep_rows
    places = [[2, 6], [5, 7], [0, 1], [4], [3]]

    def body(index_ref, *refs):
        ins, outs = refs[: 4 * len(parts)], refs[4 * len(parts) :]
        received, pair, inner, hidden = [
            jnp.concatenate([ins[4 * p + i][0] for p in range(len(parts))], 0) for i in range(4)
        ]
        wide, deep = dot_tn(received, inner).astype(BF), dot_tn(hidden, pair).astype(BF)
        for out, shards in zip(outs, places):
            for i, c in enumerate(shards):
                out[0, i * size : i * size + shard, :] = wide[c * shard : (c + 1) * shard]
                for q in range(8):
                    out[0, i * size + shard : (i + 1) * size, q * part : (q + 1) * part] = deep[
                        q * deep_rows : (q + 1) * deep_rows, c * part : (c + 1) * part
                    ]

    step = lambda i, *_: (i, 0, 0)
    flat = [a for p in parts for a in p]
    shapes = [(len(n) * size, width) for n in places]
    return call(
        body,
        (count,),
        [spec((1,) + a.shape[1:], step) for a in flat],
        [spec((1,) + n, step) for n in shapes],
        [shape_of((count,) + n, BF) for n in shapes],
        [],
        (index, *flat),
        len(parts) * count * slots * width * FF * 6,
        len(flat) * count * slots * 2 << 10,
        after=after,
    )


def halves_of(ref):
    rows = ref.shape[1] // 2
    return ref[0, :rows, :], ref[0, rows:, :]


def carry_on(index, from_x, from_y, keep_y, keep_x, after=()):
    def body(index_ref, x_ref, y_ref, keep_y_ref, keep_x_ref, upper_ref, lower_ref):
        upper_ref[0] = add(keep_y_ref[0], halves_of(x_ref)[1]).astype(BF)
        lower_ref[0] = add(keep_x_ref[0], halves_of(y_ref)[1]).astype(BF)

    args = (from_x, from_y, keep_y, keep_x)
    step = lambda i, *_: (i, 0, 0)
    return call(
        body,
        (from_x.shape[0],),
        [spec((1,) + a.shape[1:], step) for a in args],
        [spec((1,) + keep_y.shape[1:], step)] * 2,
        [shape_of(keep_y.shape, BF)] * 2,
        [],
        (index, *args),
        1024,
        1024,
        after=after,
    )


def finish(index, own, from_x, from_y, last_y, last_x, by_core, after=()):
    rows, width = own.shape[1:]
    half = rows // 2

    def body(index_ref, own_ref, x_ref, y_ref, last_y_ref, last_x_ref, *outs):
        top, low = halves_of(own_ref)
        top = add(top, halves_of(x_ref)[0]) + last_y_ref[0].astype(F32)
        low = add(low, halves_of(y_ref)[0]) + last_x_ref[0].astype(F32)
        if not by_core:
            outs[0][0, :half, :] = top.astype(BF)
            outs[0][0, half:, :] = low.astype(BF)
            return
        first = index_ref[1] == 0
        outs[0][0] = jnp.where(first, top, low).astype(BF)
        outs[1][0] = jnp.where(first, low, top).astype(BF)

    args = (own, from_x, from_y, last_y, last_x)
    step = lambda i, *_: (i, 0, 0)
    shapes = [(half, width)] * 2 if by_core else [(rows, width)]
    return call(
        body,
        (own.shape[0],),
        [spec((1,) + a.shape[1:], step) for a in args],
        [spec((1,) + n, step) for n in shapes],
        [shape_of((own.shape[0],) + n, BF) for n in shapes],
        [],
        (index, *args),
        1024,
        1024,
        after=after,
    )


class Reduce:
    def __init__(self, index, pieces):
        send_x, send_y, self.own, self.keep_y, self.keep_x = pieces
        self.index = index
        self.from_x, self.from_y = plane_swap(send_x, 2), plane_swap(send_y, 4)

    def middle(self, *after):
        self.upper, self.lower = carry_on(
            self.index, self.from_x, self.from_y, self.keep_y, self.keep_x, after
        )
        return (self.upper, self.lower)

    def end(self, by_core, *after):
        last_y, last_x = plane_swap(self.upper, 4), plane_swap(self.lower, 2)
        return finish(
            self.index, self.own, self.from_x, self.from_y, last_y, last_x, by_core, after
        )


def fold(index, even, got, after=()):
    rows, width = even.shape[1:]
    half = rows // 2

    def body(index_ref, even_ref, got_ref, send_x, send_y, own, keep_y, keep_x):
        total = [add(even_ref[i], got_ref[i]).astype(BF) for i in range(4)]
        own[0] = total[0]
        send_x[0, :half, :], send_x[0, half:, :] = total[1][:half], total[3][:half]
        send_y[0, :half, :], send_y[0, half:, :] = total[2][half:], total[3][half:]
        keep_y[0], keep_x[0] = total[2][:half], total[1][half:]

    shapes = [(1, rows, width)] * 3 + [(1, half, width)] * 2
    return call(
        body,
        (1,),
        [spec(even.shape)] * 2,
        [spec(n) for n in shapes],
        [shape_of(n, BF) for n in shapes],
        [],
        (index, even, got),
        1024,
        1024,
        after=after,
    )


def unpack(index, mines, gots, shard, after=()):
    chunks, size = len(mines), mines[0].shape[0]
    count = chunks * size
    width = mines[0].shape[2]
    deep_rows = FF // 8

    def body(index_ref, *refs):
        gate_ref, up_ref, down_ref = refs[2 * chunks :]
        step = pl.program_id(0)
        other = jnp.where(step // count == index_ref[1], 0, 1)

        def put(ref):
            value = ref[0].astype(F32)
            gate_ref[0] = value[:shard, :FF]
            up_ref[0] = value[:shard, FF:]
            for q in range(8):
                down_ref[0, q * deep_rows : (q + 1) * deep_rows, :] = value[
                    shard:, q * shard : (q + 1) * shard
                ]

        for i, ref in enumerate(refs[: 2 * chunks]):
            mine = (other == i // chunks) & ((step % count) // size == i % chunks)
            pl.when(mine)(lambda ref=ref: put(ref))

    def take(i):
        def block(e, index):
            other = jnp.where(e // count == index[1], 0, 1)
            mine = (other == i // chunks) & ((e % count) // size == i % chunks)
            return (jnp.where(mine, e % size, 0), 0, 0)

        return block

    step = lambda e, *_: (e, 0, 0)
    shapes = [(shard, FF), (shard, FF), (FF, shard)]
    return call(
        body,
        (2 * count,),
        [spec((1,) + a.shape[1:], take(i)) for i, a in enumerate((*mines, *gots))],
        [spec((1,) + n, step) for n in shapes],
        [shape_of((2 * count,) + n, F32) for n in shapes],
        [],
        (index, *mines, *gots),
        1024,
        1024,
        after=after,
    )


def combine(index, side, grads, micro, runs, sources, senses=None, got=None, after=()):
    rows, width = grads.shape[2] - 16, grads.shape[3]
    chunks, steps = len(sources), len(runs)
    counts = [a.shape[0] for a in sources]
    total = sum(counts)
    senses = list(senses or ())
    tall = rows + 16 if senses else rows
    extra = [] if got is None else [got]

    def body(index_ref, *refs):
        slots_in, refs = [r.at[0, 0] for r in refs[:steps]], refs[steps:]
        pairs_in, refs = refs[:chunks], refs[chunks:]
        sens_in, refs = refs[: len(senses)], refs[len(senses) :]
        got_in, (out_ref, table, choice) = refs[: len(extra)], refs[len(extra) :]
        step = pl.program_id(0)
        first = index_ref[3]

        def fetch(k):
            for i in range(total):
                row = expert_row(slots_in[k], 0, rows, first + i, 0)
                choice[i * PAD : (i + 1) * PAD, :] = slots_of(row, PAD).astype(BF)

        for k in range(steps):
            pl.when(step == k)(lambda k=k: fetch(k))
        flat = jnp.concatenate(
            [a[...].reshape(n * PAD, width) for a, n in zip(pairs_in, counts)], 0
        )
        value = dot_tn(choice[...], flat)
        if got_in:
            value = value + got_in[0][0, :rows, :].astype(F32)
        out_ref[0, :rows, :] = value.astype(BF)
        if not senses:
            return
        table[...] = got_in[0][0, rows:, :].astype(F32) if got_in else jnp.zeros_like(table)
        i = 0
        for ref, n in zip(sens_in, counts):
            for e in range(n):
                line = ref[e, 0, side : side + 1, :]
                high = line.astype(BF).astype(F32)
                expert = first + i
                lane = (expert // 16) * rows
                for value, base in ((high, 0), (line - high, 2 * rows)):
                    table[pl.ds(expert % 16, 1), pl.ds(pl.multiple_of(lane + base, rows), rows)] = (
                        value
                    )
                i += 1
        out_ref[0, rows:, :] = table[...].astype(BF)

    block = spec((1, tall, width), lambda k, *_: (k, 0, 0))
    return call(
        body,
        (steps,),
        run_specs(grads.shape, micro, runs, rows // 16, 16)[::2]
        + [spec((n, PAD, width), lambda k, *_: (0, 2 * k + side, 0)) for n in counts]
        + [spec((a.shape[0], 1, 2, rows), lambda k, *_: (0, k, 0, 0)) for a in senses]
        + [block] * len(extra),
        block,
        shape_of((steps, tall, width), BF),
        [pltpu.VMEM((16, width), F32), pltpu.VMEM((total * PAD, rows), BF)],
        (index, *([grads] * steps), *sources, *senses, *extra),
        1024,
        1024,
        after=after,
    )


def hidden_back(index, parts, hidden, gains, probs, cotangent, second, chips, after=()):
    rows, width = hidden.shape
    part = width // chips

    def body(
        index_ref, hidden_ref, gains_ref, probs_ref, cotangent_ref, second_ref, parts_ref,
        hidden_grad_ref, branch_ref, attended_ref, logit_ref, norm_ref, total_ref,
    ):
        chip = index_ref[0]
        total = 0.0
        for i in range(parts.shape[0]):
            total = total + parts_ref[i].astype(F32)
        total_ref[...] = total
        tail = total[rows:]
        tail = tail[:, : 2 * rows] + tail[:, 2 * rows :]
        sens = jnp.concatenate(
            [tail[:, :rows], tail[:, rows:], jnp.zeros((128 - EXPERTS, rows), F32)], 0
        ).T
        probs = probs_ref[...]
        logit_grad = probs * (sens - jnp.sum(probs * sens, -1, keepdims=True))
        logit_grad = logit_grad.astype(BF)
        logit_ref[...] = logit_grad
        moved = jnp.concatenate(
            [total_ref[:rows, lanes(j ^ chip, part)] for j in range(chips)], 1
        )
        moe_grad = moved + dot_nt(logit_grad, second_ref[:, width:])
        hidden = hidden_ref[...]
        factor = inverse_rms(hidden)
        normed = hidden * factor
        norm_ref[...] = jnp.sum(moe_grad * normed, 0, keepdims=True)
        scaled = moe_grad * gains_ref[1:2, :]
        hidden_grad = cotangent_ref[...].astype(F32) + factor * (
            scaled - normed * jnp.mean(scaled * normed, -1, keepdims=True)
        )
        hidden_grad_ref[...] = hidden_grad
        branch = (RESIDUAL_MULT * hidden_grad).astype(BF)
        branch_ref[...] = branch
        attended_ref[...] = dot_nt(branch, second_ref[:, :width]).astype(BF)

    args = (index, hidden, gains, probs, cotangent, second, parts)
    shapes = [((rows, width), F32), ((rows, width), BF), ((rows, width), BF)]
    shapes += [((rows, 128), BF), ((1, width), F32)]
    return call(
        body,
        (1,),
        [spec(a.shape) for a in args[1:]],
        [spec(n) for n, _ in shapes],
        [shape_of(n, kind) for n, kind in shapes],
        [pltpu.VMEM((rows + 16, width), F32)],
        args,
        2 * rows * width * width,
        8 << 20,
        after=after,
    )


def input_back(index, query_grad, kv_parts, tokens, first, gains, hidden_grad, cosine, sine, after=()):
    rows, width = tokens.shape
    queries, keys = H * HD, KVH * HD
    columns = queries + 2 * keys
    count = len(kv_parts)

    def body(
        index_ref, query_ref, tokens_ref, first_ref, gains_ref, hidden_ref, cosine_ref, sine_ref, *refs
    ):
        kv_refs = refs[:count]
        input_ref, low_ref, norm_ref = refs[count:]
        cos, sin = cosine_ref[...], -sine_ref[...]
        low_ref[:, :queries] = query_ref[...]
        key = sum(r[:, :keys].astype(F32) for r in kv_refs)
        for j in range(keys // 128):
            turned = rope(key[:, j * 128 : (j + 1) * 128], cos, sin)
            low_ref[:, queries + j * 128 : queries + (j + 1) * 128] = turned.astype(BF)
        value = sum(r[:, keys:].astype(F32) for r in kv_refs)
        low_ref[:, queries + keys :] = value.astype(BF)
        sens = dot_nt(low_ref[...], first_ref[:, :columns])
        values = tokens_ref[...].astype(F32)
        factor = inverse_rms(values)
        normed = values * factor
        norm_ref[...] = jnp.sum(sens * normed, 0, keepdims=True)
        scaled = sens * gains_ref[:1, :]
        input_ref[...] = (
            hidden_ref[...]
            + factor * (scaled - normed * jnp.mean(scaled * normed, -1, keepdims=True))
        ).astype(BF)

    args = (index, query_grad, tokens, first, gains, hidden_grad, cosine, sine, *kv_parts)
    return call(
        body,
        (1,),
        [spec(a.shape) for a in args[1:]],
        [spec((rows, width)), spec((rows, columns)), spec((1, width))],
        [shape_of((rows, width), BF), shape_of((rows, columns), BF), shape_of((1, width), F32)],
        [],
        args,
        2 * rows * width * columns,
        8 << 20,
        after=after,
    )


def dense_grads(index, shards, lefts, rights, gains, router_lefts, router_rights, after=()):
    width = lefts[0].shape[1]
    rows, columns = lefts[0].shape[0], rights[0].shape[1]
    count, extra = len(lefts), len(router_lefts)
    part = max(width // shards, 128)
    steps = width // part

    def body(index_ref, *refs):
        left = jnp.concatenate([r[...] for r in refs[:count]], 0)
        right = jnp.concatenate([r[...] for r in refs[count : 2 * count]], 0)
        gain = sum(r[...] for r in refs[2 * count : 3 * count])
        even_ref, odd_ref = refs[-2:]
        gain = jnp.broadcast_to(gain, (128, part)).T
        got = dot_tn(left, right).astype(BF)
        if extra:
            left = jnp.concatenate([r[...] for r in refs[3 * count : 3 * count + extra]], 0)
            right = jnp.concatenate([r[...] for r in refs[3 * count + extra : -2]], 0)
            lane = lax.broadcasted_iota(jnp.int32, gain.shape, 1)
            gain = jnp.where(lane < EXPERTS, dot_tn(left, right), gain)

        def put(ref):
            ref[0, :, :columns] = got
            ref[0, :, columns:] = gain.astype(BF)

        odd = pl.program_id(0) % 2 == 1
        pl.when(odd)(lambda: put(odd_ref))
        pl.when(jnp.logical_not(odd))(lambda: put(even_ref))

    take = lambda j, index: (0, j ^ index[5])
    some = spec((rows, part), take)
    return call(
        body,
        (steps,),
        [some] * count
        + [spec((rows, columns))] * count
        + [spec((1, part), take)] * count
        + [some] * extra
        + [spec((rows, 128))] * extra,
        [spec((1, part, columns + 128), lambda j, *_: (j // 2, 0, 0))] * 2,
        [shape_of((steps // 2, part, columns + 128), BF)] * 2,
        [],
        (index, *lefts, *rights, *gains, *router_lefts, *router_rights),
        2 * count * rows * width * columns,
        4 * width * columns,
        after=after,
    )


def gather_pieces(own, after=None):
    along_x, along_y = plane_swap(own, 2), plane_swap(own, 4)
    if after is not None:
        along_x, along_y = lax.optimization_barrier((along_x, along_y, after))[:2]
    far = [plane_swap(halves(along_x)[0], 4), plane_swap(halves(along_y)[1], 2)]
    near = [own, along_x, along_y]
    pieces = []
    for block in near:
        pieces += [block, sibling(block)]
    return pieces + far + [sibling(block) for block in far]


def on_device(
    tokens,
    routes,
    cotangent,
    norm_one,
    norm_two,
    w_query,
    w_key,
    w_value,
    w_out,
    w_router,
    w_gate,
    w_up,
    w_down,
):
    micro_count, _, rows, width = tokens.shape
    tokens, routes, cotangent = tokens[:, 0], routes[:, 0], cotangent[:, 0]
    local_experts, shard = w_gate.shape[0], w_gate.shape[1]
    core_experts = local_experts // 2
    ctx_count, exp_count = lax.axis_size("ctx"), lax.axis_size("exp")
    plane = lax.axis_size("dp") * ctx_count
    chips = plane // 2
    fast = chips == 4 and exp_count == 4 and ctx_count == 4
    fast = fast and micro_count == 2 and core_experts % 2 == 0
    ctx = lax.axis_index("ctx")
    place = lax.axis_index("dp") * ctx_count + ctx
    chip, core, level = place // 2, place % 2, lax.axis_index("exp")
    first_expert = level * local_experts + core * core_experts
    base = place if fast else jnp.zeros_like(place)
    index = jnp.stack([chip, core, ctx, first_expert, level, base]).astype(jnp.int32)
    micros = range(micro_count)

    cosine, sine = rotation(ctx * rows, rows)
    cosine_t, sine_t = cosine.T, sine.T
    cosine_w = jnp.tile(cosine, (1, 4))
    sine_w = jnp.concatenate([-sine, sine, -sine, sine], 1)

    def beside(columns):
        return jnp.pad(columns, ((0, 0), (0, 128 - columns.shape[1])))

    dense = jnp.concatenate(
        [
            w_query, w_key, w_value, beside(jnp.stack([norm_one, norm_two], 1)),
            w_out, beside(w_router),
        ],
        1,
    )

    def later(array, *others):
        if not others:
            return array
        return lax.optimization_barrier((array,) + others)[0]

    def run_attention(m, after=()):
        attended_low[m], turned[m], stats[m] = attend(index, query[m], kv_blocks[m], after)

    def run_route(m, copies, after=()):
        hidden[m], moe_in[m], probs[m], message = route(
            index, attended_low[m], tokens[m], second, gain_rows, picks[m], chips, copies, after
        )
        return message

    def run_hidden_back(m, parts, after=()):
        hidden_grads[m], branches[m], attended_grad, logits[m], norms[m] = hidden_back(
            index, parts, hidden[m], gain_rows, probs[m], cotangent[m], second, chips, after
        )
        return attended_grad

    def run_attend_back(m, attended_grad, after=()):
        return attend_back(
            index, query[m], kv_blocks[m], attended_grad, turned[m], stats[m], cosine_t, sine_t, after
        )

    def run_input_back(m, query_grad, kv_parts, after=()):
        backs[m] = input_back(
            index, query_grad, kv_parts, tokens[m], first, gain_rows, hidden_grads[m],
            cosine_w, sine_w, after,
        )

    def finish_output(m, parts):
        total = jnp.sum(parts.astype(F32), 0)
        return (hidden[m] + RESIDUAL_MULT * reorder(total, chips, chip, 1)).astype(BF)

    def projection_grads(after=()):
        return dense_grads(
            index, plane, normed_in, [b[1] for b in backs], [b[2] for b in backs], [], [], after
        )

    def output_grads(after=()):
        return dense_grads(index, plane, attended_low, branches, norms, moe_in, logits, after)

    names = [[None] * micro_count for _ in range(12)]
    attended_low, turned, stats, hidden, moe_in, probs = names[:6]
    hidden_grads, branches, logits, norms, backs, outputs = names[6:]

    picks, message = prepare(index, routes, cotangent, chips)

    def exchange(blocks):
        return lax.all_to_all(blocks, "exp", split_axis=0, concat_axis=0, tiled=True)

    if fast:
        cotangents = lax.all_gather(message, "exp")
        half = core_experts // 2
        deep_rows = FF // 8

        swapped = sibling(pack(index, True, w_gate, w_up, w_down))
        packed = pack(index, False, w_gate, w_up, w_down)

        class Weights:
            def __init__(self, own):
                self.near = [own, plane_swap(own, 2), plane_swap(own, 4)]

            def hand_on(self, *after):
                _, x, y = self.near
                self.parts = halves(later(x, *after))[0], halves(later(y, *after))[1]
                return self.parts

            def full(self):
                a, b = self.parts
                return self.near + [plane_swap(a, 4), plane_swap(b, 2)]

        class PlaneSum:
            def __init__(self, shards, *after):
                even, self.odd = shards
                self.reduce = Reduce(index, fold(index, even, sibling(self.odd), after))

            def middle(self, *after):
                return self.reduce.middle(*after)

            def end(self, *after):
                self.total = self.reduce.end(False, *after)[0][0]
                self.at = 0
                return self.split()

            def split(self):
                bit = 1 << self.at
                lower, upper = halves(self.total)
                flag = (level & bit) != 0
                self.kept, self.sent = jnp.where(flag, upper, lower), jnp.where(flag, lower, upper)
                return (self.sent,)

            def over_exp(self, *after):
                bit = (1, 2, 2, 1)[self.at]
                got = lax.ppermute(self.sent, "exp", [(i, i ^ bit) for i in range(4)])
                got = later(got, *after)
                flag = (level & bit) != 0
                if self.at < 2:
                    self.total = add(self.kept, got).astype(BF)
                else:
                    self.total = jnp.concatenate(
                        [jnp.where(flag, got, self.total), jnp.where(flag, self.total, got)], 0
                    )
                self.at += 1
                if self.at < 2:
                    return self.split()
                self.sent = self.total
                return (self.sent,)

        def run_experts(c, m, weights, after=()):
            got[c, m] = experts(index, c * half, x_pairs[m], g_pair, m, range(4), weights, after)
            return got[c, m][4]

        def run_combine(m, kind, side, shared=None, after=()):
            pieces = [got[c, m][4:] for c in range(2)]
            senses = [p[2] for p in pieces] if kind else None
            return combine(
                index, side, g_pair[side], m, range(4), [p[kind] for p in pieces], senses, shared, after
            )

        def send_back(parts):
            far = lax.ppermute(parts[3], "ctx", [(2, 3), (3, 2)])
            return add(parts[2], far).astype(BF)

        def arrive_back(parts, along):
            near = lax.ppermute(parts[1], "ctx", [(1, 0), (3, 2)])
            return [parts[0], near, lax.ppermute(along, "ctx", [(2, 0), (3, 1)])]

        def gather_near(kv, *after):
            near = lax.ppermute(kv, "ctx", [(0, 1), (2, 3)])
            along = lax.ppermute(kv, "ctx", [(0, 2), (1, 3)])
            far = lax.ppermute(later(along, *after), "ctx", [(2, 3), (3, 2)])
            return [kv, near, along, far]

        pieces = gather_pieces(dense)
        owns = [merge(index, c * half, half, packed, swapped) for c in range(2)]
        first, second, gain_rows, query, *rest = project(index, tokens, pieces, cosine_w, sine_w)
        normed_in, kv_own = rest[:2], rest[2:]
        kv_blocks = [gather_near(kv_own[0])]
        early = Weights(later(owns[0], *pieces[6:8]))
        run_attention(0, tuple(owns))
        kv_blocks.append(gather_near(later(kv_own[1], kv_blocks[0][2]), attended_low[0]))
        handed = early.hand_on(attended_low[0])
        message = run_route(0, 4, (*kv_blocks[1][1:], *handed))
        x_all = [exchange(message)]
        run_attention(1, (message,))
        late = Weights(later(owns[1], *handed))
        g_pair = [cotangents, sibling(later(cotangents, message))]
        early_full = early.full()
        handed = late.hand_on(attended_low[1])
        message = run_route(1, 4, (g_pair[1], *early_full[3:], *handed))
        x_all.append(exchange(later(message, x_all[0])))
        x_pairs = [[x_all[0], sibling(later(x_all[0], message))]]
        got = {}
        done = run_experts(0, 0, early_full)
        late_full = late.full()
        done = run_experts(1, 0, late_full, (done,))
        in_other = run_combine(0, 1, 1, after=(done,))
        out_other = run_combine(0, 0, 1, after=(in_other,))
        in_total = run_combine(0, 1, 0, sibling(in_other), (out_other,))
        out_total = run_combine(0, 0, 0, sibling(out_other), (in_total,))
        x_pairs.append([x_all[1], sibling(later(x_all[1], in_total))])
        in_parts = [exchange(later(in_total, x_all[1]))]
        done = run_experts(0, 1, early_full, (out_total,))
        done = run_experts(1, 1, late_full, (done,))
        in_other = run_combine(1, 1, 1, after=(done,))
        grads = expert_grads(index, [got[0, m][:4] for m in micros], (in_other,))
        reducing = [Reduce(index, grads)]
        in_total = run_combine(1, 1, 0, sibling(in_other), (grads[0],))
        in_parts.append(exchange(later(in_total, in_parts[0])))
        grads = expert_grads(index, [got[1, m][:4] for m in micros], (in_total,))
        reducing.append(Reduce(index, grads))
        attended_grad = run_hidden_back(0, in_parts[0], (grads[0],))
        query_grad, *parts = run_attend_back(0, attended_grad)
        query_grads, kv_parts, along = [query_grad], [parts], [send_back(parts)]
        attended_grad = run_hidden_back(
            1, in_parts[1], (along[0],) + reducing[0].middle(query_grad)
        )
        out_parts = [exchange(later(out_total, attended_grad))]
        query_grad, *parts = run_attend_back(1, attended_grad)
        query_grads.append(query_grad)
        kv_parts.append(parts)
        along.append(send_back(parts))
        returned = arrive_back(kv_parts[0], along[0])
        out_other = run_combine(1, 0, 1, after=(query_grad, *returned[1:]))
        ends = [reducing[0].end(True, out_other)]
        run_input_back(0, query_grads[0], returned, (along[1], *ends[0]))
        gots = [sibling(ends[0][1])]
        out_total = run_combine(1, 0, 0, sibling(out_other), (backs[0][1],))
        second_shards = output_grads((out_total,))
        outputs[0] = finish_output(0, later(out_parts[0], second_shards[0]))
        step = reducing[1].middle(second_shards[1])
        run_input_back(
            1,
            query_grads[1],
            arrive_back(kv_parts[1], along[1]),
            (second_shards[0], outputs[0], *step),
        )
        out_parts.append(exchange(later(out_total, backs[1][1])))
        second_sum = PlaneSum(second_shards, backs[1][1])
        first_shards = projection_grads((second_sum.reduce.own,))
        second_sum.middle(first_shards[1])
        first_sum = PlaneSum(first_shards, second_sum.reduce.upper)
        second_sum.end(first_sum.reduce.own)
        ends.append(reducing[1].end(True, second_sum.sent[0]))
        step = first_sum.middle(*ends[1])
        gots.append(sibling(ends[1][1]))
        second_sum.over_exp(*step)
        step = first_sum.end(second_sum.sent)
        second_sum.over_exp(*step)
        gate_grad, up_grad, down_grad = unpack(
            index, [e[0] for e in ends], gots, shard, (second_sum.sent,)
        )
        step = first_sum.over_exp(second_sum.sent, gate_grad)
        second_sum.over_exp(*step)
        step = first_sum.over_exp(second_sum.sent)
        second_sum.over_exp(*step)
        step = first_sum.over_exp(second_sum.total)
        outputs[1] = finish_output(1, later(out_parts[1], *step))
        first_sum.over_exp()
        first_total, second_total = first_sum.total, second_sum.total
    else:

        def swap_in(array, axis):
            mine = lax.dynamic_slice_in_dim(array, core * core_experts, core_experts, 0)
            other = lax.dynamic_slice_in_dim(array, (1 - core) * core_experts, core_experts, 0)
            got = sibling(other)
            pair = [jnp.where(core == 0, mine, got), jnp.where(core == 0, got, mine)]
            return jnp.concatenate(pair, axis)

        def swap_out(array, axis):
            half = array.shape[axis] // 2
            mine = lax.dynamic_slice_in_dim(array, core * half, half, axis)
            other = lax.dynamic_slice_in_dim(array, (1 - core) * half, half, axis)
            got = sibling(other.astype(BF)).astype(F32)
            pair = [jnp.where(core == 0, mine, got), jnp.where(core == 0, got, mine)]
            return jnp.concatenate(pair, 0)

        def whole(array):
            blocks = lax.all_gather(array, PLANE)
            return [blocks[j] for j in range(plane)]

        first, second, gain_rows, query, *rest = project(
            index, tokens, whole(dense), cosine_w, sine_w
        )
        normed_in, kv_own = rest[:micro_count], rest[micro_count:]
        weights = [
            jnp.concatenate(gather_chips(later(swap_in(a, axis), first)), axis)
            for a, axis in ((jnp.concatenate([w_gate, w_up], 2), 1), (w_down, 2))
        ]
        kv_blocks, last = [None] * micro_count, first
        gate_up_grad, down_grad = 0.0, 0.0
        group = min(exp_count, 4)
        for m in micros:
            kv_blocks[m] = gather_ctx(later(kv_own[m], last))
            run_attention(m)
            g_all = lax.all_gather(later(message[m : m + 1], last), "exp")
            g_pair = [g_all, sibling(g_all)]
            x_all = lax.all_gather(run_route(m, 1)[0], "exp")
            x_pair = [x_all, sibling(x_all)]
            parts_of = [[], []]
            for g in range(0, exp_count, group):
                runs = range(g, g + group)
                *kept, out, back, sens = experts(
                    index, 0, x_pair, g_pair, 0, runs, weights, (last,)
                )
                gate_up_grad += jnp.einsum(
                    "esd,esf->edf", kept[0], kept[2], preferred_element_type=F32
                )
                down_grad += jnp.einsum("esf,esd->efd", kept[3], kept[1], preferred_element_type=F32)
                for i, source in enumerate((out, back)):
                    sides = [None, None]
                    for side in (1, 0):
                        sides[side] = last = combine(
                            index, side, g_pair[side], 0, runs, [source], [sens] if i else None,
                            sibling(sides[1]) if side == 0 else None, (last,),
                        )
                    parts_of[i].append(last)
            homes = [exchange(jnp.concatenate(parts, 0)) for parts in parts_of]
            outputs[m] = finish_output(m, homes[0])
            last = outputs[m]
            attended_grad = run_hidden_back(m, homes[1])
            query_grad, *parts = run_attend_back(m, attended_grad)
            run_input_back(m, query_grad, [reduce_ctx(parts).astype(BF)])
        gate_up_grad = swap_out(reduce_chips(jnp.split(gate_up_grad.astype(BF), chips, 1)), 1)
        gate_grad, up_grad = gate_up_grad[..., :FF], gate_up_grad[..., FF:]
        down_grad = swap_out(reduce_chips(jnp.split(down_grad.astype(BF), chips, 2)), 2)

        def plane_sum(shards):
            total = jnp.stack(shards, 1)
            total = total.reshape(width, total.shape[-1])
            return lax.psum(lax.psum_scatter(total, PLANE, scatter_dimension=0, tiled=True), "exp")

        first_total, second_total = plane_sum(projection_grads()), plane_sum(output_grads())

    first_total, second_total = first_total.astype(F32), second_total.astype(F32)
    cuts = [H * HD, (H + KVH) * HD, (H + 2 * KVH) * HD]
    query_grad, key_grad, value_grad, norm_one_grad = jnp.split(first_total, cuts, 1)
    return (
        jnp.stack(outputs)[:, None],
        jnp.stack([b[0] for b in backs])[:, None],
        norm_one_grad[:, 0],
        second_total[:, width + EXPERTS],
        query_grad,
        key_grad,
        value_grad,
        second_total[:, :width],
        second_total[:, width : width + EXPERTS],
        gate_grad,
        up_grad,
        down_grad,
    )


def solution(mesh):
    rows = P(None, ("dp", "exp"), "ctx", None)
    row_shard = P(PLANE, None)
    return jax.shard_map(
        on_device,
        mesh=mesh,
        in_specs=(
            rows,
            rows,
            rows,
            P(PLANE),
            P(PLANE),
            row_shard,
            row_shard,
            row_shard,
            row_shard,
            row_shard,
            P("exp", PLANE, None),
            P("exp", PLANE, None),
            P("exp", None, PLANE),
        ),
        out_specs=(
            rows,
            rows,
            P(PLANE),
            P(PLANE),
            row_shard,
            row_shard,
            row_shard,
            row_shard,
            row_shard,
            P("exp", PLANE, None),
            P("exp", PLANE, None),
            P("exp", None, PLANE),
        ),
        check_vma=False,
    )
```

```python
import jax
import jax.numpy as jnp
from jax import lax
from jax.experimental import pallas as pl
from jax.experimental.pallas import tpu as pltpu
from jax.sharding import PartitionSpec as P

H = 16
KVH = 8
HD = 64
EXPERTS = 32
FF = 512
TOPK = 8
BLOCK = 256
CAP = 72
PAD = 80
GROUP = H // KVH

EPSILON = 1e-06
BASE_THETA = 10000.0
NEGATIVE = -1e30
ATTENTION_MULT = 0.015625
RESIDUAL_MULT = 0.22

PLANE = ("dp", "ctx")
BF = jnp.bfloat16
F32 = jnp.float32


def dot(left, right):
    return jnp.dot(left, right, preferred_element_type=F32)


def dot_tn(left, right):
    return lax.dot_general(left, right, (((0,), (0,)), ((), ())), preferred_element_type=F32)


def dot_nt(left, right):
    return lax.dot_general(left, right, (((1,), (1,)), ((), ())), preferred_element_type=F32)


def add(left, right):
    return left.astype(F32) + right.astype(F32)


def relative(blocks, index):
    count = len(blocks)
    bit = 1
    while bit < count:
        on = (index & bit) != 0
        blocks = [jnp.where(on, blocks[j ^ bit], blocks[j]) for j in range(count)]
        bit *= 2
    return blocks


def reorder(array, count, index, axis):
    return jnp.concatenate(relative(jnp.split(array, count, axis), index), axis)


def plane_swap(array, mask):
    count = lax.axis_size("dp") * lax.axis_size("ctx")
    return lax.ppermute(array, PLANE, [(i, i ^ mask) for i in range(count)])


def sibling(array):
    return plane_swap(array, 1)


def halves(array):
    return jnp.split(array, 2, -2)


def gather_chips(own):
    chips = lax.axis_size("dp") * lax.axis_size("ctx") // 2
    if chips == 4:
        along_x, along_y = plane_swap(own, 2), plane_swap(own, 4)
        first, last = halves(along_x)[0], halves(along_y)[1]
        far = jnp.concatenate([plane_swap(first, 4), plane_swap(last, 2)], -2)
        return [own, along_x, along_y, far]
    blocks, mask = [own], 1
    while mask < chips:
        blocks = blocks + [plane_swap(b, 2 * mask) for b in blocks]
        mask *= 2
    return blocks


def gather_plane(own):
    blocks = []
    for block in gather_chips(own):
        blocks += [block, sibling(block)]
    return blocks


def reduce_chips(blocks):
    chips = len(blocks)
    if chips == 4:
        upper, lower = zip(*[halves(b) for b in blocks])
        from_x = plane_swap(jnp.concatenate([upper[1], upper[3]], -2), 2)
        from_y = plane_swap(jnp.concatenate([lower[2], lower[3]], -2), 4)
        x_own, x_rest = halves(from_x)
        y_own, y_rest = halves(from_y)
        upper_last = plane_swap(add(upper[2], x_rest).astype(BF), 4)
        lower_last = plane_swap(add(lower[1], y_rest).astype(BF), 2)
        top = add(upper[0], x_own) + upper_last.astype(F32)
        low = add(lower[0], y_own) + lower_last.astype(F32)
        return jnp.concatenate([top, low], -2)
    mask = chips // 2
    while mask:
        blocks = [
            add(blocks[j], plane_swap(blocks[j + mask], 2 * mask)).astype(BF) for j in range(mask)
        ]
        mask //= 2
    return blocks[0].astype(F32)


def reduce_plane(blocks):
    other = sibling(jnp.concatenate(blocks[1::2], -2))
    others = jnp.split(other, len(blocks) // 2, -2)
    return reduce_chips([add(a, b).astype(BF) for a, b in zip(blocks[0::2], others)])


def gather_ctx(own):
    count = lax.axis_size("ctx")
    if count == 4:
        near = lax.ppermute(own, "ctx", [(0, 1), (2, 3)])
        along = lax.ppermute(own, "ctx", [(0, 2), (1, 3)])
        far = lax.ppermute(along, "ctx", [(2, 3), (3, 2)])
        return [own, near, along, far]
    blocks, mask = [own], 1
    while mask < count:
        blocks = blocks + [
            lax.ppermute(b, "ctx", [(i, i ^ mask) for i in range(count)]) for b in blocks
        ]
        mask *= 2
    return blocks


def reduce_ctx(blocks):
    count = lax.axis_size("ctx")
    if count == 4:
        far = lax.ppermute(blocks[3], "ctx", [(2, 3), (3, 2)])
        along = lax.ppermute(add(blocks[2], far).astype(BF), "ctx", [(2, 0), (3, 1)])
        near = lax.ppermute(blocks[1], "ctx", [(1, 0), (3, 2)])
        return add(blocks[0], near) + along.astype(F32)
    mask = count // 2
    while mask:
        perm = [(i, i ^ mask) for i in range(count)]
        blocks = [
            add(blocks[j], lax.ppermute(blocks[j + mask], "ctx", perm)).astype(BF)
            for j in range(mask)
        ]
        mask //= 2
    return blocks[0].astype(F32)


def ring_step(array):
    count = lax.axis_size("exp")
    return lax.ppermute(array, "exp", [(i, (i + 1) % count) for i in range(count)])


def gather_ring(own):
    blocks = [own]
    for _ in range(lax.axis_size("exp") - 1):
        blocks.append(ring_step(blocks[-1]))
    return blocks


def reduce_ring(blocks):
    count = len(blocks)
    total = blocks[1 % count]
    for k in range(2, count + 1):
        total = add(ring_step(total), blocks[k % count]).astype(BF)
    return total


def rotation(offset, row_count):
    half_size = HD // 2
    inverse = jnp.exp(jnp.arange(half_size, dtype=F32) * (-2.0 * jnp.log(F32(BASE_THETA)) / HD))
    places = (offset + jnp.arange(row_count, dtype=jnp.int32)).astype(F32)
    angles = places[:, None] * inverse[None, :]
    return (jnp.cos(angles), jnp.sin(angles))


def rope(pair, cosine, sine):
    lane = lax.broadcasted_iota(jnp.int32, pair.shape, 1)
    former = lane % HD < HD // 2
    turned = jnp.where(
        former, pltpu.roll(pair, 2 * HD - HD // 2, 1), pltpu.roll(pair, HD // 2, 1)
    )
    return pair * cosine + turned * sine


def inverse_rms(values):
    return lax.rsqrt(jnp.mean(values * values, -1, keepdims=True) + EPSILON)


def of_micro(array, m):
    return pl.BlockSpec((1,) + array.shape[1:], lambda *_: (m,) + (0,) * (array.ndim - 1))


def spec(shape, index=None):
    index = index or (lambda *_: (0,) * len(shape))
    return pl.BlockSpec(shape, index)


def once(shape, index=None):
    index = index or (lambda *_: (0,) * len(shape))
    return pl.BlockSpec(shape, index, pipeline_mode=pl.Buffered(1))


def shape_of(shape, kind):
    return jax.ShapeDtypeStruct(shape, kind)


COST = {
    "prepare": 4, "pack": 4, "merge": 3, "project": 10, "attend": 17, "attend_back": 20, "route": 5, "experts": 18,
    "expert_grads": 14, "combine": 6, "carry_on": 4, "finish": 5, "bundle": 2, "fold": 3, "unpack": 8, "hidden_back": 6,
    "input_back": 6, "dense_grads": 9, "total_of": 5,
}


def call(
    body, grid, in_specs, out_specs, out_shape, scratch, args, flops, moved, limit=56, after=()
):
    count, first = len(after), len(args)

    def ordered(*refs):
        body(*refs[:first], *refs[first + count :])

    return pl.pallas_call(
        ordered,
        grid_spec=pltpu.PrefetchScalarGridSpec(
            num_scalar_prefetch=1,
            grid=grid,
            in_specs=list(in_specs) + [pl.BlockSpec(memory_space=pl.ANY)] * count,
            out_specs=out_specs,
            scratch_shapes=scratch,
        ),
        out_shape=out_shape,
        compiler_params=pltpu.CompilerParams(vmem_limit_bytes=limit << 20),
        cost_estimate=pl.CostEstimate(
            flops=int(COST[body.__qualname__.split(".")[0]] * 6.921e+09), bytes_accessed=1024, transcendentals=0
        ),
    )(*args, *after)


def lanes(index, size):
    return pl.ds(pl.multiple_of(index * size, size), size)


def shards_of(pieces, rows):
    found, j = [], 0
    for piece in pieces:
        if piece.shape[0] == rows:
            found.append((j, 0))
            j += 1
        else:
            found.append((j, 0) if not found or found[-1][0] != j else (j, rows // 2))
            j += found[-1][1] > 0
    return found


def fill(scratch, refs, base, rows):
    for ref, (j, row) in zip(refs, shards_of(refs, rows)):
        count = ref.shape[0]
        at = pl.multiple_of((j ^ base) * rows + row, count)
        scratch[pl.ds(at, count), :] = ref[...]


def bundle(index, parts, gains, second, router):
    rows = second.shape[0]

    def body(index_ref, *refs):
        *part_refs, first_ref, last_ref, second_ref, router_ref, out_ref = refs
        at = 0
        for ref in part_refs:
            out_ref[:, at : at + ref.shape[1]] = ref[...]
            at += ref.shape[1]
        blank = jnp.zeros((126, rows), F32)
        gain_rows = [r[...].astype(F32) for r in (first_ref, last_ref)]
        out_ref[:, at : at + 128] = jnp.concatenate(gain_rows + [blank], 0).T.astype(BF)
        at += 128
        out_ref[:, at : at + second_ref.shape[1]] = second_ref[...]
        at += second_ref.shape[1]
        out_ref[:, at:] = router_ref[...]

    args = (*parts, *gains, second, router)
    size = (rows, sum(a.shape[1] for a in parts) + 128 + second.shape[1] + 128)
    return call(
        body,
        (1,),
        [spec(a.shape) for a in args],
        spec(size),
        shape_of(size, BF),
        [],
        (index, *args),
        1024,
        1024,
    )


def prepare(index, routes, cotangent, chips, after=()):
    micro, rows, width = cotangent.shape
    part = width // chips

    def body(index_ref, routes_ref, cotangent_ref, picks_ref, message_ref):
        chip = index_ref[0]
        earlier = lax.broadcasted_iota(jnp.int32, (rows, rows), 0) > lax.broadcasted_iota(
            jnp.int32, (rows, rows), 1
        )
        earlier = jnp.where(earlier, 1.0, 0.0).astype(BF)
        expert = lax.broadcasted_iota(jnp.int32, (rows, 128), 1)
        for m in range(micro):
            chosen = routes_ref[m]
            pick = jnp.zeros((rows, 128), F32)
            for k in range(TOPK):
                pick = pick + jnp.where(chosen[:, k : k + 1] == expert, 1.0, 0.0)
            rank = dot(earlier, pick.astype(BF))
            slot = jnp.where((pick > 0.0) & (rank < CAP), rank, -1.0).T
            picks_ref[m] = pick
            out = message_ref.at[m]
            for j in range(chips):
                out[:rows, j * part : (j + 1) * part] = cotangent_ref[m, :, lanes(j ^ chip, part)]
            out[rows:, :] = jnp.concatenate(
                [slot[:16], slot[16:32], jnp.zeros((16, width - 2 * rows), F32)], 1
            ).astype(BF)

    message = (micro, rows + 16, width)
    return call(
        body,
        (1,),
        [spec(routes.shape), spec(cotangent.shape)],
        [spec((micro, rows, 128)), spec(message)],
        [shape_of((micro, rows, 128), F32), shape_of(message, BF)],
        [],
        (index, routes, cotangent),
        1 << 26,
        4 << 20,
        after=after,
    )


def project(index, tokens, pieces, cosine, sine, after=()):
    micro, rows, width = tokens.shape
    shard = pieces[0].shape[0]
    columns = pieces[0].shape[1]
    queries, keys = H * HD, KVH * HD
    inner = queries + 2 * keys + 128
    count = len(pieces)

    def body(index_ref, tokens_ref, cosine_ref, sine_ref, *refs):
        weight, second_ref, gains_ref, *rest = refs[count:]
        query_refs, normed_refs, kv_refs = rest[:micro], rest[micro : 2 * micro], rest[2 * micro :]
        fill(weight, [r.at[:, :inner] for r in refs[:count]], index_ref[5], shard)
        fill(second_ref, [r.at[:, inner:] for r in refs[:count]], index_ref[5], shard)
        gains_ref[...] = weight[:, inner - 128 :].astype(F32).T[:8]
        gain = gains_ref[:1, :]
        cos, sin = cosine_ref[...], sine_ref[...]
        for m in range(micro):
            values = tokens_ref[m].astype(F32)
            normed = (values * inverse_rms(values) * gain).astype(BF)
            normed_refs[m][...] = normed
            for j in range(queries // 256):
                got = dot(normed, weight[:, j * 256 : (j + 1) * 256])
                for i in range(2):
                    turned = rope(got[:, i * 128 : (i + 1) * 128], cos, sin)
                    at = j * 256 + i * 128
                    query_refs[m][:, at : at + 128] = turned.astype(BF)
            for j in range(keys // 256):
                got = dot(normed, weight[:, queries + j * 256 : queries + (j + 1) * 256])
                for i in range(2):
                    turned = rope(got[:, i * 128 : (i + 1) * 128], cos, sin)
                    at = j * 256 + i * 128
                    kv_refs[m][:, at : at + 128] = turned.astype(BF)
            got = dot(normed, weight[:, queries + keys : queries + 2 * keys])
            kv_refs[m][:, keys:] = got.astype(BF)

    shapes = [((width, inner), BF), ((width, columns - inner), BF), ((8, width), F32)]
    shapes += [((rows, queries), BF)] * micro
    shapes += [((rows, width), BF)] * micro + [((rows, 2 * keys), BF)] * micro
    return call(
        body,
        (1,),
        [spec(a.shape) for a in (tokens, cosine, sine, *pieces)],
        [spec(n) for n, _ in shapes],
        [shape_of(n, kind) for n, kind in shapes],
        [],
        (index, tokens, cosine, sine, *pieces),
        2 * micro * rows * width * columns,
        12 << 20,
        after=after,
    )


def place_heads(pair, which):
    lane = lax.broadcasted_iota(jnp.int32, pair.shape, 1)
    mine = (lane < HD) if which == 0 else (lane >= HD)
    moved = pltpu.roll(pair, HD, 1)
    both = (pair, moved) if which == 0 else (moved, pair)
    return jnp.concatenate([jnp.where(mine, b, 0.0) for b in both], 0)


def attend(index, query, blocks, after=()):
    rows = query.shape[0]
    count = len(blocks)
    steps = KVH // 2
    width = H * HD

    def body(index_ref, query_ref, *refs):
        key_refs, value_refs = refs[:count], refs[count : 2 * count]
        low_ref, turned_ref, stat_ref = refs[2 * count : 2 * count + 3]
        top, total, mixed = refs[2 * count + 3 :]
        ctx = index_ref[2]
        heads = []
        for a in range(2):
            pair = query_ref[:, a * 128 : (a + 1) * 128].astype(F32) * ATTENTION_MULT
            heads.append(place_heads(pair, a).T.astype(BF))

        def visit(j):
            key, value = key_refs[j][...], value_refs[j][...]
            for a in range(2):
                scores = dot(key, heads[a])
                peak = jnp.max(scores, 0, keepdims=True)
                if j:
                    peak = jnp.maximum(peak, top[a])
                expo = jnp.exp(scores - peak)
                added = jnp.sum(expo, 0, keepdims=True)
                got = dot_tn(value, expo.astype(BF))[a * HD : (a + 1) * HD]
                if j:
                    scale = jnp.exp(top[a] - peak)
                    added = added + total[a] * scale
                    got = got + mixed[a] * scale
                top[a] = peak
                total[a] = added
                mixed[a] = got

        visit(0)
        for j in range(1, count):
            pl.when((ctx ^ j) <= ctx)(lambda j=j: visit(j))
        for a in range(2):
            got = mixed[a] / total[a]
            turned = jnp.concatenate([got[:, :rows], got[:, rows:]], 0)
            turned_ref[a * 128 : (a + 1) * 128, :] = turned
            low_ref[:, a * 128 : (a + 1) * 128] = turned.T.astype(BF)
            stat_ref[0, a : a + 1, :] = top[a] + jnp.log(total[a])

    keys = [spec((rows, 128), lambda i, *_: (0, i))] * count
    values = [spec((rows, 128), lambda i, *_: (0, i + steps))] * count
    return call(
        body,
        (steps,),
        [spec((rows, 256), lambda i, *_: (0, i))] + keys + values,
        [
            spec((rows, 256), lambda i, *_: (0, i)),
            spec((256, rows), lambda i, *_: (i, 0)),
            spec((1, 2, 2 * rows), lambda i, *_: (i, 0, 0)),
        ],
        [
            shape_of((rows, width), BF),
            shape_of((width, rows), F32),
            shape_of((steps, 2, 2 * rows), F32),
        ],
        [
            pltpu.VMEM((2, 1, 2 * rows), F32),
            pltpu.VMEM((2, 1, 2 * rows), F32),
            pltpu.VMEM((2, HD, 2 * rows), F32),
        ],
        (index, query, *blocks, *blocks),
        8 * rows * rows * count * width,
        6 << 20,
        after=after,
    )


def attend_back(index, query, blocks, attended_grad, attended, stats, cosine, sine, after=()):
    rows = query.shape[0]
    count = len(blocks)
    steps = KVH // 2
    half = HD // 2

    def body(index_ref, query_ref, grad_ref, attended_ref, stat_ref, cosine_ref, sine_ref, *refs):
        key_refs, value_refs = refs[:count], refs[count : 2 * count]
        query_out, kv_out = refs[2 * count], refs[2 * count + 1 : 3 * count + 1]
        (query_sum,) = refs[3 * count + 1 :]
        ctx = index_ref[2]
        step = pl.program_id(0)
        heads, grads, heads_t, grads_t, deltas = [], [], [], [], []
        for a in range(2):
            at = slice(a * 128, (a + 1) * 128)
            placed = place_heads(query_ref[:, at].astype(F32) * ATTENTION_MULT, a)
            heads.append(placed.astype(BF))
            heads_t.append(placed.T.astype(BF))
            pair = grad_ref[:, at].astype(F32)
            placed = place_heads(pair, a)
            grads.append(placed.astype(BF))
            grads_t.append(placed.T.astype(BF))
            product = pair.T * attended_ref[at, :]
            deltas.append(
                jnp.concatenate(
                    [jnp.sum(product[i * HD : (i + 1) * HD], 0, keepdims=True) for i in range(2)], 1
                )
            )

        def visit(j):
            key, value = key_refs[j][...], value_refs[j][...]
            key_sum, value_sum = 0.0, 0.0
            for a in range(2):
                probs = jnp.exp(dot(key, heads_t[a]) - stat_ref[0, a : a + 1, :])
                score_grad = (probs * (dot(value, grads_t[a]) - deltas[a])).astype(BF)
                key_sum = key_sum + dot(score_grad, heads[a])
                value_sum = value_sum + dot(probs.astype(BF), grads[a])
                got = dot_tn(key, score_grad)[a * HD : (a + 1) * HD]
                if j:
                    got = got + query_sum[a]
                query_sum[a] = got
            kv_out[j][:, lanes(step, 128)] = key_sum.astype(BF)
            kv_out[j][:, lanes(step + steps, 128)] = value_sum.astype(BF)

        visit(0)
        for j in range(1, count):
            reach = (ctx ^ j) <= ctx
            pl.when(reach)(lambda j=j: visit(j))

            @pl.when(jnp.logical_not(reach) & (step == 0))
            def _(j=j):
                kv_out[j][...] = jnp.zeros_like(kv_out[j])

        cos, sin = cosine_ref[...], sine_ref[...]
        for a in range(2):
            got = query_sum[a] * ATTENTION_MULT
            pieces = []
            for i in range(2):
                former = got[:half, i * rows : (i + 1) * rows]
                latter = got[half:, i * rows : (i + 1) * rows]
                pieces += [former * cos + latter * sin, latter * cos - former * sin]
            query_out[:, a * 128 : (a + 1) * 128] = jnp.concatenate(pieces, 0).T.astype(BF)

    wide = spec((rows, 256), lambda i, *_: (0, i))
    keys = [spec((rows, 128), lambda i, *_: (0, i))] * count
    values = [spec((rows, 128), lambda i, *_: (0, i + steps))] * count
    kv = (rows, 2 * KVH * HD)
    return call(
        body,
        (steps,),
        [
            wide,
            wide,
            spec((256, rows), lambda i, *_: (i, 0)),
            spec((1, 2, 2 * rows), lambda i, *_: (i, 0, 0)),
            spec(cosine.shape),
            spec(sine.shape),
        ]
        + keys
        + values,
        [wide] + [spec(kv)] * count,
        [shape_of((rows, H * HD), BF)] + [shape_of(kv, BF)] * count,
        [pltpu.VMEM((2, HD, 2 * rows), F32)],
        (index, query, attended_grad, attended, stats, cosine, sine, *blocks, *blocks),
        20 * rows * rows * count * H * HD,
        8 << 20,
        after=after,
    )


def route(index, m, attended, tokens, second, gains, picks, chips, copies, after=()):
    rows, width = attended.shape
    part = width // chips

    def body(
        index_ref, attended_ref, tokens_ref, second_ref, gains_ref, picks_ref,
        hidden_ref, moe_ref, probs_ref, message_ref,
    ):
        chip = index_ref[0]
        hidden = tokens_ref[0].astype(F32) + RESIDUAL_MULT * dot(
            attended_ref[...], second_ref[:, :width]
        )
        hidden_ref[...] = hidden
        moe_in = (hidden * inverse_rms(hidden) * gains_ref[1:2, :]).astype(BF)
        moe_ref[...] = moe_in
        picked = picks_ref[0] > 0.0
        chosen = jnp.where(picked, dot(moe_in, second_ref[:, width:]), NEGATIVE)
        expo = jnp.where(picked, jnp.exp(chosen - jnp.max(chosen, -1, keepdims=True)), 0.0)
        probs = expo / jnp.sum(expo, -1, keepdims=True)
        probs_ref[...] = probs
        turned = probs.T
        high = turned.astype(BF).astype(F32)
        low = turned - high
        tail = jnp.concatenate([high[:16], high[16:32], low[:16], low[16:32]], 1).astype(BF)
        for i in range(copies):
            for j in range(chips):
                message_ref[i, :rows, j * part : (j + 1) * part] = moe_ref[:, lanes(j ^ chip, part)]
            message_ref[i, rows:, :] = tail

    args = (index, attended, tokens, second, gains, picks)
    shapes = [((rows, width), F32), ((rows, width), BF), ((rows, 128), F32)]
    shapes += [((copies, rows + 16, width), BF)]
    return call(
        body,
        (1,),
        [of_micro(a, m) if a.ndim == 3 else spec(a.shape) for a in args[1:]],
        [spec(n) for n, _ in shapes],
        [shape_of(n, kind) for n, kind in shapes],
        [],
        args,
        2 * rows * width * width,
        6 << 20,
        after=after,
    )


def pack(index, other, w_gate, w_up, w_down, after=()):
    count, shard = w_gate.shape[0] // 2, w_gate.shape[1]
    deep_rows = FF // 8

    def body(index_ref, gate_ref, up_ref, down_ref, out_ref):
        out_ref[0, :shard, :FF] = gate_ref[0]
        out_ref[0, :shard, FF:] = up_ref[0]
        for q in range(8):
            out_ref[0, shard:, q * shard : (q + 1) * shard] = down_ref[
                0, q * deep_rows : (q + 1) * deep_rows, :
            ]

    def take(i, index):
        core = 1 - index[1] if other else index[1]
        return (core * count + i, 0, 0)

    size = (shard + deep_rows, 2 * FF)
    return call(
        body,
        (count,),
        [spec((1,) + a.shape[1:], take) for a in (w_gate, w_up, w_down)],
        spec((1,) + size, lambda i, *_: (i, 0, 0)),
        shape_of((count,) + size, BF),
        [],
        (index, w_gate, w_up, w_down),
        1024,
        1024,
        after=after,
    )


def merge(index, first, count, mine, got, after=()):
    rows, width = mine.shape[1:]

    def body(index_ref, mine_ref, got_ref, out_ref):
        core = index_ref[1]
        out_ref[0, pl.ds(pl.multiple_of(core * rows, rows), rows), :] = mine_ref[0]
        out_ref[0, pl.ds(pl.multiple_of((1 - core) * rows, rows), rows), :] = got_ref[0]

    some = spec((1, rows, width), lambda i, *_: (first + i, 0, 0))
    return call(
        body,
        (count,),
        [some, some],
        spec((1, 2 * rows, width), lambda i, *_: (i, 0, 0)),
        shape_of((count, 2 * rows, width), BF),
        [],
        (index, mine, got),
        1024,
        1024,
        after=after,
    )


def total_of(index, left, right, after=()):
    def body(index_ref, left_ref, right_ref, out_ref):
        out_ref[...] = add(left_ref[...], right_ref[...]).astype(BF)

    some = spec((1,) + left.shape[1:], lambda i, *_: (i, 0, 0))
    return call(
        body,
        (left.shape[0],),
        [some, some],
        some,
        shape_of(left.shape, BF),
        [],
        (index, left, right),
        1024,
        1024,
        after=after,
    )


def expert_row(ref, start, rows, expert, first):
    table = ref[start : start + 16, pl.ds(pl.multiple_of((expert // 16) * rows + first, rows), rows)]
    table = table.astype(F32)
    line = lax.broadcasted_iota(jnp.int32, table.shape, 0) == expert % 16
    return jnp.sum(jnp.where(line, table, 0.0), 0, keepdims=True)


def slots_of(row, count=CAP):
    slot = lax.broadcasted_iota(jnp.int32, (count, row.shape[1]), 0).astype(F32)
    return jnp.where(slot == row, 1.0, 0.0)


def run_specs(shape, micro, runs, first, count):
    if len(shape) == 3:
        return [once((1, count, shape[2]), lambda *_, k=k: (k, first, 0)) for k in runs for _ in range(2)]
    return [
        once((1, 1, count, shape[3]), lambda *_, k=k: (k, micro, first, 0))
        for k in runs
        for _ in range(2)
    ]


def experts(index, offset, token_pair, grad_pair, micro, runs, weights, after=()):
    count = weights[0].shape[0]
    total = 2 * len(runs)
    rows, width = token_pair[0].shape[1] - 16, token_pair[0].shape[2]
    slots, padded = total * CAP, total * PAD
    pieces = len(weights)
    packed = pieces == 5
    shard, deep_rows, part = width // 8, FF // 8, width // 8

    def body(index_ref, *refs):
        tokens_in = [r.at[0] for r in refs[:total]]
        grads_in = [r.at[0, 0] for r in refs[total : 2 * total]]
        at = 2 * total
        weights_in = refs[at : at + pieces]
        at += pieces
        received_ref, pair_ref, inner_ref, hidden_ref, out_ref, back_ref, sens_ref = refs[at : at + 7]
        received, grads, probs_at, *whole = refs[at + 7 :]
        step = pl.program_id(0)

        @pl.when(step == 0)
        def _():
            for k in range(0, total, 2):
                found = []
                for r in (k, k + 1):
                    takes, probs = [], []
                    for i in range(count):
                        expert = index_ref[3] + offset + i
                        take = slots_of(expert_row(grads_in[r], rows, rows, expert, 0))
                        prob = expert_row(tokens_in[r], rows, rows, expert, 0) + expert_row(
                            tokens_in[r], rows, rows, expert, 2 * rows
                        )
                        takes.append(take)
                        probs.append(jnp.sum(take * prob, 1, keepdims=True))
                    take = jnp.concatenate(takes, 0).astype(BF)
                    found.append(
                        (dot(take, tokens_in[r][:rows, :]), dot(take, grads_in[r][:rows, :]), probs)
                    )
                for i in range(count):
                    span = slice(k * CAP, (k + 2) * CAP)
                    pick = slice(i * CAP, (i + 1) * CAP)
                    received[i, span, :] = jnp.concatenate([f[0][pick] for f in found], 0).astype(BF)
                    grads[i, span, :] = jnp.concatenate([f[1][pick] for f in found], 0).astype(BF)
                    prob = jnp.concatenate([f[2][i] for f in found], 0)
                    probs_at[i, span, :] = jnp.broadcast_to(prob, (2 * CAP, 128))

        if packed:
            wide, deep = whole
            own, along_x, along_y, *far = [r.at[0] for r in weights_in]
            size = shard + deep_rows
            for c in range(8):
                if c < 6:
                    source = (own, along_x, along_y)[c // 2].at[(c % 2) * size : (c % 2 + 1) * size]
                else:
                    source = far[c - 6]
                wide[c * shard : (c + 1) * shard, :] = source[:shard, :]
                for q in range(8):
                    deep[q * deep_rows : (q + 1) * deep_rows, c * part : (c + 1) * part] = source[
                        shard:, q * part : (q + 1) * part
                    ]
        else:
            wide, deep = [r.at[0] for r in weights_in]

        rows_in = received[step]
        received_ref[0] = rows_in
        prob = probs_at[step][:, :1]
        scaled = RESIDUAL_MULT * grads[step].astype(F32)
        pair = (prob * scaled).astype(BF)
        pair_ref[0] = pair
        both = dot(rows_in, wide[...])
        gate_h, up_h = both[:, :FF], both[:, FF:]
        sigma = jax.nn.sigmoid(gate_h)
        silu_gate = gate_h * sigma
        hidden = (silu_gate * up_h).astype(BF)
        hidden_ref[0] = hidden
        inner = dot_nt(pair, deep[...])
        gate_d = (inner * up_h * sigma * (1.0 + gate_h * (1.0 - sigma))).astype(BF)
        up_d = (inner * silu_gate).astype(BF)
        inner_ref[0, :, :FF] = gate_d
        inner_ref[0, :, FF:] = up_d
        out = dot(hidden, deep[...]).astype(BF).astype(F32)

        def put(ref, value):
            blank = jnp.zeros((PAD - CAP, width), F32)
            for r in range(total):
                run = jnp.concatenate([value[r * CAP : (r + 1) * CAP], blank], 0)
                ref[0, r * PAD : (r + 1) * PAD, :] = run.astype(BF)

        put(out_ref, prob * out)
        sens = jnp.sum(out * scaled, 1, keepdims=True)
        expert = index_ref[3] + offset + step
        for r in range(total):
            take = slots_of(expert_row(grads_in[r], rows, rows, expert, 0))
            sens_ref[0, r // 2, r % 2 : r % 2 + 1, :] = jnp.sum(
                take * sens[r * CAP : (r + 1) * CAP], 0, keepdims=True
            )
        put(back_ref, dot_nt(inner_ref[0], wide[...]))

    step = lambda i, *_: (i, 0, 0)
    sizes = [(slots, n) for n in (width, width, 2 * FF, FF)] + [(padded, width)] * 2
    run_in = [
        n for pair in (token_pair, grad_pair) for n in run_specs(pair[0].shape, micro, runs, 0, rows + 16)
    ]
    return call(
        body,
        (count,),
        run_in + [spec((1,) + a.shape[1:], step) for a in weights],
        [spec((1,) + n, step) for n in sizes]
        + [spec((1, total // 2, 2, rows), lambda i, *_: (i, 0, 0, 0))],
        [shape_of((count,) + n, BF) for n in sizes]
        + [shape_of((count, total // 2, 2, rows), F32)],
        [
            pltpu.VMEM((count, slots, width), BF),
            pltpu.VMEM((count, slots, width), BF),
            pltpu.VMEM((count, slots, 128), F32),
        ]
        + ([pltpu.VMEM((width, 2 * FF), BF), pltpu.VMEM((FF, width), BF)] if packed else []),
        (index, *(list(token_pair) * len(runs)), *(list(grad_pair) * len(runs)), *weights),
        count * slots * width * FF * 16,
        count * slots * 14 << 10,
        60,
        after,
    )


def expert_grads(index, parts, after=()):
    count, slots, width = parts[0][0].shape
    shard, deep_rows, part = width // 8, FF // 8, width // 8
    size = shard + deep_rows
    places = [[2, 6], [5, 7], [0, 1], [4], [3]]

    def body(index_ref, *refs):
        ins, outs = refs[: 4 * len(parts)], refs[4 * len(parts) :]
        received, pair, inner, hidden = [
            jnp.concatenate([ins[4 * p + i][0] for p in range(len(parts))], 0) for i in range(4)
        ]
        wide, deep = dot_tn(received, inner).astype(BF), dot_tn(hidden, pair).astype(BF)
        for out, shards in zip(outs, places):
            for i, c in enumerate(shards):
                out[0, i * size : i * size + shard, :] = wide[c * shard : (c + 1) * shard]
                for q in range(8):
                    out[0, i * size + shard : (i + 1) * size, q * part : (q + 1) * part] = deep[
                        q * deep_rows : (q + 1) * deep_rows, c * part : (c + 1) * part
                    ]

    step = lambda i, *_: (i, 0, 0)
    flat = [a for p in parts for a in p]
    shapes = [(len(n) * size, width) for n in places]
    return call(
        body,
        (count,),
        [spec((1,) + a.shape[1:], step) for a in flat],
        [spec((1,) + n, step) for n in shapes],
        [shape_of((count,) + n, BF) for n in shapes],
        [],
        (index, *flat),
        len(parts) * count * slots * width * FF * 6,
        len(flat) * count * slots * 2 << 10,
        after=after,
    )


def halves_of(ref):
    rows = ref.shape[1] // 2
    return ref[0, :rows, :], ref[0, rows:, :]


def carry_on(index, from_x, from_y, keep_y, keep_x, after=()):
    def body(index_ref, x_ref, y_ref, keep_y_ref, keep_x_ref, upper_ref, lower_ref):
        upper_ref[0] = add(keep_y_ref[0], halves_of(x_ref)[1]).astype(BF)
        lower_ref[0] = add(keep_x_ref[0], halves_of(y_ref)[1]).astype(BF)

    args = (from_x, from_y, keep_y, keep_x)
    step = lambda i, *_: (i, 0, 0)
    return call(
        body,
        (from_x.shape[0],),
        [spec((1,) + a.shape[1:], step) for a in args],
        [spec((1,) + keep_y.shape[1:], step)] * 2,
        [shape_of(keep_y.shape, BF)] * 2,
        [],
        (index, *args),
        1024,
        1024,
        after=after,
    )


def finish(index, own, from_x, from_y, last_y, last_x, by_core, after=()):
    rows, width = own.shape[1:]
    half = rows // 2

    def body(index_ref, own_ref, x_ref, y_ref, last_y_ref, last_x_ref, *outs):
        top, low = halves_of(own_ref)
        top = add(top, halves_of(x_ref)[0]) + last_y_ref[0].astype(F32)
        low = add(low, halves_of(y_ref)[0]) + last_x_ref[0].astype(F32)
        if not by_core:
            outs[0][0, :half, :] = top.astype(BF)
            outs[0][0, half:, :] = low.astype(BF)
            return
        first = index_ref[1] == 0
        outs[0][0] = jnp.where(first, top, low).astype(BF)
        outs[1][0] = jnp.where(first, low, top).astype(BF)

    args = (own, from_x, from_y, last_y, last_x)
    step = lambda i, *_: (i, 0, 0)
    shapes = [(half, width)] * 2 if by_core else [(rows, width)]
    return call(
        body,
        (own.shape[0],),
        [spec((1,) + a.shape[1:], step) for a in args],
        [spec((1,) + n, step) for n in shapes],
        [shape_of((own.shape[0],) + n, BF) for n in shapes],
        [],
        (index, *args),
        1024,
        1024,
        after=after,
    )


class Reduce:
    def __init__(self, index, pieces):
        send_x, send_y, self.own, self.keep_y, self.keep_x = pieces
        self.index = index
        self.from_x, self.from_y = plane_swap(send_x, 2), plane_swap(send_y, 4)

    def middle(self, *after):
        self.upper, self.lower = carry_on(
            self.index, self.from_x, self.from_y, self.keep_y, self.keep_x, after
        )
        return (self.upper, self.lower)

    def end(self, by_core, *after):
        last_y, last_x = plane_swap(self.upper, 4), plane_swap(self.lower, 2)
        return finish(
            self.index, self.own, self.from_x, self.from_y, last_y, last_x, by_core, after
        )


def fold(index, even, got, after=()):
    rows, width = even.shape[1:]
    half = rows // 2

    def body(index_ref, even_ref, got_ref, send_x, send_y, own, keep_y, keep_x):
        total = [add(even_ref[i], got_ref[i]).astype(BF) for i in range(4)]
        own[0] = total[0]
        send_x[0, :half, :], send_x[0, half:, :] = total[1][:half], total[3][:half]
        send_y[0, :half, :], send_y[0, half:, :] = total[2][half:], total[3][half:]
        keep_y[0], keep_x[0] = total[2][:half], total[1][half:]

    shapes = [(1, rows, width)] * 3 + [(1, half, width)] * 2
    return call(
        body,
        (1,),
        [spec(even.shape)] * 2,
        [spec(n) for n in shapes],
        [shape_of(n, BF) for n in shapes],
        [],
        (index, even, got),
        1024,
        1024,
        after=after,
    )


def unpack(index, mines, gots, shard, after=()):
    chunks, size = len(mines), mines[0].shape[0]
    count = chunks * size
    width = mines[0].shape[2]
    deep_rows = FF // 8

    def body(index_ref, *refs):
        gate_ref, up_ref, down_ref = refs[2 * chunks :]
        step = pl.program_id(0)
        other = jnp.where(step // count == index_ref[1], 0, 1)

        def put(ref):
            value = ref[0].astype(F32)
            gate_ref[0] = value[:shard, :FF]
            up_ref[0] = value[:shard, FF:]
            for q in range(8):
                down_ref[0, q * deep_rows : (q + 1) * deep_rows, :] = value[
                    shard:, q * shard : (q + 1) * shard
                ]

        for i, ref in enumerate(refs[: 2 * chunks]):
            mine = (other == i // chunks) & ((step % count) // size == i % chunks)
            pl.when(mine)(lambda ref=ref: put(ref))

    def take(i):
        def block(e, index):
            other = jnp.where(e // count == index[1], 0, 1)
            mine = (other == i // chunks) & ((e % count) // size == i % chunks)
            return (jnp.where(mine, e % size, 0), 0, 0)

        return block

    step = lambda e, *_: (e, 0, 0)
    shapes = [(shard, FF), (shard, FF), (FF, shard)]
    return call(
        body,
        (2 * count,),
        [spec((1,) + a.shape[1:], take(i)) for i, a in enumerate((*mines, *gots))],
        [spec((1,) + n, step) for n in shapes],
        [shape_of((2 * count,) + n, F32) for n in shapes],
        [],
        (index, *mines, *gots),
        1024,
        1024,
        after=after,
    )


def combine(index, side, grads, micro, runs, sources, senses=None, got=None, after=()):
    rows, width = grads.shape[2] - 16, grads.shape[3]
    chunks, steps = len(sources), len(runs)
    counts = [a.shape[0] for a in sources]
    total = sum(counts)
    senses = list(senses or ())
    tall = rows + 16 if senses else rows
    extra = [] if got is None else [got]

    def body(index_ref, *refs):
        slots_in, refs = [r.at[0, 0] for r in refs[:steps]], refs[steps:]
        pairs_in, refs = refs[:chunks], refs[chunks:]
        sens_in, refs = refs[: len(senses)], refs[len(senses) :]
        got_in, (out_ref, table, choice) = refs[: len(extra)], refs[len(extra) :]
        step = pl.program_id(0)
        first = index_ref[3]

        def fetch(k):
            for i in range(total):
                row = expert_row(slots_in[k], 0, rows, first + i, 0)
                choice[i * PAD : (i + 1) * PAD, :] = slots_of(row, PAD).astype(BF)

        for k in range(steps):
            pl.when(step == k)(lambda k=k: fetch(k))
        flat = jnp.concatenate(
            [a[...].reshape(n * PAD, width) for a, n in zip(pairs_in, counts)], 0
        )
        value = dot_tn(choice[...], flat)
        if got_in:
            value = value + got_in[0][0, :rows, :].astype(F32)
        out_ref[0, :rows, :] = value.astype(BF)
        if not senses:
            return
        table[...] = got_in[0][0, rows:, :].astype(F32) if got_in else jnp.zeros_like(table)
        i = 0
        for ref, n in zip(sens_in, counts):
            for e in range(n):
                line = ref[e, 0, side : side + 1, :]
                high = line.astype(BF).astype(F32)
                expert = first + i
                lane = (expert // 16) * rows
                for value, base in ((high, 0), (line - high, 2 * rows)):
                    table[pl.ds(expert % 16, 1), pl.ds(pl.multiple_of(lane + base, rows), rows)] = (
                        value
                    )
                i += 1
        out_ref[0, rows:, :] = table[...].astype(BF)

    block = spec((1, tall, width), lambda k, *_: (k, 0, 0))
    return call(
        body,
        (steps,),
        run_specs(grads.shape, micro, runs, rows // 16, 16)[::2]
        + [spec((n, PAD, width), lambda k, *_: (0, 2 * k + side, 0)) for n in counts]
        + [spec((a.shape[0], 1, 2, rows), lambda k, *_: (0, k, 0, 0)) for a in senses]
        + [block] * len(extra),
        block,
        shape_of((steps, tall, width), BF),
        [pltpu.VMEM((16, width), F32), pltpu.VMEM((total * PAD, rows), BF)],
        (index, *([grads] * steps), *sources, *senses, *extra),
        1024,
        1024,
        after=after,
    )


def hidden_back(index, m, parts, hidden, gains, probs, cotangent, second, chips, after=()):
    rows, width = hidden.shape
    part = width // chips

    def body(
        index_ref, hidden_ref, gains_ref, probs_ref, cotangent_ref, second_ref, parts_ref,
        hidden_grad_ref, branch_ref, attended_ref, logit_ref, norm_ref, total_ref,
    ):
        chip = index_ref[0]
        total = 0.0
        for i in range(parts.shape[0]):
            total = total + parts_ref[i].astype(F32)
        total_ref[...] = total
        tail = total[rows:]
        tail = tail[:, : 2 * rows] + tail[:, 2 * rows :]
        sens = jnp.concatenate(
            [tail[:, :rows], tail[:, rows:], jnp.zeros((128 - EXPERTS, rows), F32)], 0
        ).T
        probs = probs_ref[...]
        logit_grad = probs * (sens - jnp.sum(probs * sens, -1, keepdims=True))
        logit_grad = logit_grad.astype(BF)
        logit_ref[...] = logit_grad
        moved = jnp.concatenate(
            [total_ref[:rows, lanes(j ^ chip, part)] for j in range(chips)], 1
        )
        moe_grad = moved + dot_nt(logit_grad, second_ref[:, width:])
        hidden = hidden_ref[...]
        factor = inverse_rms(hidden)
        normed = hidden * factor
        norm_ref[...] = jnp.sum(moe_grad * normed, 0, keepdims=True)
        scaled = moe_grad * gains_ref[1:2, :]
        hidden_grad = cotangent_ref[0].astype(F32) + factor * (
            scaled - normed * jnp.mean(scaled * normed, -1, keepdims=True)
        )
        hidden_grad_ref[...] = hidden_grad
        branch = (RESIDUAL_MULT * hidden_grad).astype(BF)
        branch_ref[...] = branch
        attended_ref[...] = dot_nt(branch, second_ref[:, :width]).astype(BF)

    args = (index, hidden, gains, probs, cotangent, second, parts)
    shapes = [((rows, width), F32), ((rows, width), BF), ((rows, width), BF)]
    shapes += [((rows, 128), BF), ((1, width), F32)]
    return call(
        body,
        (1,),
        [of_micro(a, m) if a is cotangent else spec(a.shape) for a in args[1:]],
        [spec(n) for n, _ in shapes],
        [shape_of(n, kind) for n, kind in shapes],
        [pltpu.VMEM((rows + 16, width), F32)],
        args,
        2 * rows * width * width,
        8 << 20,
        after=after,
    )


def input_back(index, m, query_grad, kv_parts, tokens, first, gains, hidden_grad, cosine, sine, after=()):
    rows, width = tokens.shape[1:]
    queries, keys = H * HD, KVH * HD
    columns = queries + 2 * keys
    count = len(kv_parts)

    def body(
        index_ref, query_ref, tokens_ref, first_ref, gains_ref, hidden_ref, cosine_ref, sine_ref, *refs
    ):
        kv_refs = refs[:count]
        input_ref, low_ref, norm_ref = refs[count:]
        cos, sin = cosine_ref[...], -sine_ref[...]
        low_ref[:, :queries] = query_ref[...]
        key = sum(r[:, :keys].astype(F32) for r in kv_refs)
        for j in range(keys // 128):
            turned = rope(key[:, j * 128 : (j + 1) * 128], cos, sin)
            low_ref[:, queries + j * 128 : queries + (j + 1) * 128] = turned.astype(BF)
        value = sum(r[:, keys:].astype(F32) for r in kv_refs)
        low_ref[:, queries + keys :] = value.astype(BF)
        sens = dot_nt(low_ref[...], first_ref[:, :columns])
        values = tokens_ref[0].astype(F32)
        factor = inverse_rms(values)
        normed = values * factor
        norm_ref[...] = jnp.sum(sens * normed, 0, keepdims=True)
        scaled = sens * gains_ref[:1, :]
        input_ref[...] = (
            hidden_ref[...]
            + factor * (scaled - normed * jnp.mean(scaled * normed, -1, keepdims=True))
        ).astype(BF)

    args = (index, query_grad, tokens, first, gains, hidden_grad, cosine, sine, *kv_parts)
    return call(
        body,
        (1,),
        [of_micro(a, m) if a is tokens else spec(a.shape) for a in args[1:]],
        [spec((rows, width)), spec((rows, columns)), spec((1, width))],
        [shape_of((rows, width), BF), shape_of((rows, columns), BF), shape_of((1, width), F32)],
        [],
        args,
        2 * rows * width * columns,
        8 << 20,
        after=after,
    )


def dense_grads(index, shards, lefts, rights, gains, router_lefts, router_rights, after=()):
    width = lefts[0].shape[1]
    rows, columns = lefts[0].shape[0], rights[0].shape[1]
    count, extra = len(lefts), len(router_lefts)
    part = max(width // shards, 128)
    steps = width // part

    def body(index_ref, *refs):
        left = jnp.concatenate([r[...] for r in refs[:count]], 0)
        right = jnp.concatenate([r[...] for r in refs[count : 2 * count]], 0)
        gain = sum(r[...] for r in refs[2 * count : 3 * count])
        even_ref, odd_ref = refs[-2:]
        gain = jnp.broadcast_to(gain, (128, part)).T
        got = dot_tn(left, right).astype(BF)
        if extra:
            left = jnp.concatenate([r[...] for r in refs[3 * count : 3 * count + extra]], 0)
            right = jnp.concatenate([r[...] for r in refs[3 * count + extra : -2]], 0)
            lane = lax.broadcasted_iota(jnp.int32, gain.shape, 1)
            gain = jnp.where(lane < EXPERTS, dot_tn(left, right), gain)

        def put(ref):
            ref[0, :, :columns] = got
            ref[0, :, columns:] = gain.astype(BF)

        odd = pl.program_id(0) % 2 == 1
        pl.when(odd)(lambda: put(odd_ref))
        pl.when(jnp.logical_not(odd))(lambda: put(even_ref))

    take = lambda j, index: (0, j ^ index[5])
    some = spec((rows, part), take)
    return call(
        body,
        (steps,),
        [some] * count
        + [spec((rows, columns))] * count
        + [spec((1, part), take)] * count
        + [some] * extra
        + [spec((rows, 128))] * extra,
        [spec((1, part, columns + 128), lambda j, *_: (j // 2, 0, 0))] * 2,
        [shape_of((steps // 2, part, columns + 128), BF)] * 2,
        [],
        (index, *lefts, *rights, *gains, *router_lefts, *router_rights),
        2 * count * rows * width * columns,
        4 * width * columns,
        after=after,
    )


def gather_pieces(own, after=None):
    along_x, along_y = plane_swap(own, 2), plane_swap(own, 4)
    if after is not None:
        along_x, along_y = lax.optimization_barrier((along_x, along_y, after))[:2]
    far = [plane_swap(halves(along_x)[0], 4), plane_swap(halves(along_y)[1], 2)]
    near = [own, along_x, along_y]
    pieces = []
    for block in near:
        pieces += [block, sibling(block)]
    return pieces + far + [sibling(block) for block in far]


def on_device(
    tokens,
    routes,
    cotangent,
    norm_one,
    norm_two,
    w_query,
    w_key,
    w_value,
    w_out,
    w_router,
    w_gate,
    w_up,
    w_down,
):
    micro_count, _, rows, width = tokens.shape
    tokens, routes, cotangent = tokens[:, 0], routes[:, 0], cotangent[:, 0]
    local_experts, shard = w_gate.shape[0], w_gate.shape[1]
    core_experts = local_experts // 2
    ctx_count, exp_count = lax.axis_size("ctx"), lax.axis_size("exp")
    plane = lax.axis_size("dp") * ctx_count
    chips = plane // 2
    fast = chips == 4 and exp_count == 4 and ctx_count == 4
    fast = fast and micro_count == 2 and core_experts % 2 == 0
    ctx = lax.axis_index("ctx")
    place = lax.axis_index("dp") * ctx_count + ctx
    chip, core, level = place // 2, place % 2, lax.axis_index("exp")
    first_expert = level * local_experts + core * core_experts
    base = place if fast else jnp.zeros_like(place)
    index = jnp.stack([chip, core, ctx, first_expert, level, base]).astype(jnp.int32)
    micros = range(micro_count)

    cosine, sine = rotation(ctx * rows, rows)
    cosine_t, sine_t = cosine.T, sine.T
    cosine_w = jnp.tile(cosine, (1, 4))
    sine_w = jnp.concatenate([-sine, sine, -sine, sine], 1)

    def beside(columns):
        return jnp.pad(columns, ((0, 0), (0, 128 - columns.shape[1])))

    projections = [w_query, w_key, w_value]
    if fast:
        dense = bundle(
            index, projections, [norm_one[None], norm_two[None]], w_out, beside(w_router)
        )
    else:
        gains = beside(jnp.stack([norm_one, norm_two], 1))
        dense = jnp.concatenate([*projections, gains, w_out, beside(w_router)], 1)

    def later(array, *others):
        if not others:
            return array
        return lax.optimization_barrier((array,) + others)[0]

    def run_attention(m, after=()):
        attended_low[m], turned[m], stats[m] = attend(index, query[m], kv_blocks[m], after)

    def run_route(m, copies, after=()):
        hidden[m], moe_in[m], probs[m], message = route(
            index, m, attended_low[m], tokens, second, gain_rows, picks, chips, copies, after
        )
        return message

    def run_hidden_back(m, parts, after=()):
        hidden_grads[m], branches[m], attended_grad, logits[m], norms[m] = hidden_back(
            index, m, parts, hidden[m], gain_rows, probs[m], cotangent, second, chips, after
        )
        return attended_grad

    def run_attend_back(m, attended_grad, after=()):
        return attend_back(
            index, query[m], kv_blocks[m], attended_grad, turned[m], stats[m], cosine_t, sine_t, after
        )

    def run_input_back(m, query_grad, kv_parts, after=()):
        backs[m] = input_back(
            index, m, query_grad, kv_parts, tokens, first, gain_rows, hidden_grads[m],
            cosine_w, sine_w, after,
        )

    def finish_output(m, parts):
        total = jnp.sum(parts.astype(F32), 0)
        return (hidden[m] + RESIDUAL_MULT * reorder(total, chips, chip, 1)).astype(BF)

    def projection_grads(after=()):
        return dense_grads(
            index, plane, normed_in, [b[1] for b in backs], [b[2] for b in backs], [], [], after
        )

    def output_grads(after=()):
        return dense_grads(index, plane, attended_low, branches, norms, moe_in, logits, after)

    names = [[None] * micro_count for _ in range(12)]
    attended_low, turned, stats, hidden, moe_in, probs = names[:6]
    hidden_grads, branches, logits, norms, backs, outputs = names[6:]

    picks, message = prepare(index, routes, cotangent, chips, (dense,))

    def exchange(blocks):
        return lax.all_to_all(blocks, "exp", split_axis=0, concat_axis=0, tiled=True)

    if fast:
        cotangents = lax.all_gather(message, "exp")
        half = core_experts // 2
        deep_rows = FF // 8

        swapped = sibling(pack(index, True, w_gate, w_up, w_down))
        packed = pack(index, False, w_gate, w_up, w_down)

        class Weights:
            def __init__(self, own):
                self.near = [own, plane_swap(own, 2), plane_swap(own, 4)]

            def hand_on(self, *after):
                _, x, y = self.near
                self.parts = halves(later(x, *after))[0], halves(later(y, *after))[1]
                return self.parts

            def full(self):
                a, b = self.parts
                return self.near + [plane_swap(a, 4), plane_swap(b, 2)]

        class PlaneSum:
            def __init__(self, shards, *after):
                even, self.odd = shards
                self.reduce = Reduce(index, fold(index, even, sibling(self.odd), after))

            def middle(self, *after):
                return self.reduce.middle(*after)

            def end(self, *after):
                self.total = self.reduce.end(False, *after)[0][0]
                self.at = 0
                return self.split()

            def split(self):
                bit = 1 << self.at
                lower, upper = halves(self.total)
                flag = (level & bit) != 0
                self.kept, self.sent = jnp.where(flag, upper, lower), jnp.where(flag, lower, upper)
                return (self.sent,)

            def over_exp(self, *after):
                bit = (1, 2, 2, 1)[self.at]
                got = lax.ppermute(self.sent, "exp", [(i, i ^ bit) for i in range(4)])
                got = later(got, *after)
                flag = (level & bit) != 0
                if self.at < 2:
                    self.total = add(self.kept, got).astype(BF)
                else:
                    self.total = jnp.concatenate(
                        [jnp.where(flag, got, self.total), jnp.where(flag, self.total, got)], 0
                    )
                self.at += 1
                if self.at < 2:
                    return self.split()
                self.sent = self.total
                return (self.sent,)

        def run_experts(c, m, weights, after=()):
            got[c, m] = experts(index, c * half, x_pairs[m], g_pair, m, range(4), weights, after)
            return got[c, m][4]

        def run_combine(m, kind, side, shared=None, after=()):
            pieces = [got[c, m][4:] for c in range(2)]
            senses = [p[2] for p in pieces] if kind else None
            return combine(
                index, side, g_pair[side], m, range(4), [p[kind] for p in pieces], senses, shared, after
            )

        def send_back(parts):
            far = lax.ppermute(parts[3], "ctx", [(2, 3), (3, 2)])
            return add(parts[2], far).astype(BF)

        def arrive_back(parts, along):
            near = lax.ppermute(parts[1], "ctx", [(1, 0), (3, 2)])
            return [parts[0], near, lax.ppermute(along, "ctx", [(2, 0), (3, 1)])]

        def gather_near(kv, *after):
            near = lax.ppermute(kv, "ctx", [(0, 1), (2, 3)])
            along = lax.ppermute(kv, "ctx", [(0, 2), (1, 3)])
            far = lax.ppermute(later(along, *after), "ctx", [(2, 3), (3, 2)])
            return [kv, near, along, far]

        pieces = gather_pieces(dense)
        owns = [merge(index, c * half, half, packed, swapped) for c in range(2)]
        first, second, gain_rows, *rest = project(index, tokens, pieces, cosine_w, sine_w)
        query, normed_in, kv_own = rest[:2], rest[2:4], rest[4:]
        kv_blocks = [gather_near(kv_own[0])]
        early = Weights(later(owns[0], *pieces[6:8]))
        run_attention(0, tuple(owns))
        kv_blocks.append(gather_near(later(kv_own[1], kv_blocks[0][2]), attended_low[0]))
        handed = early.hand_on(attended_low[0])
        message = run_route(0, 4, (*kv_blocks[1][1:], *handed))
        x_all = [exchange(message)]
        run_attention(1, (message,))
        late = Weights(later(owns[1], *handed))
        g_pair = [cotangents, sibling(later(cotangents, message))]
        early_full = early.full()
        handed = late.hand_on(attended_low[1])
        message = run_route(1, 4, (g_pair[1], *early_full[3:], *handed))
        x_all.append(exchange(later(message, x_all[0])))
        x_pairs = [[x_all[0], sibling(later(x_all[0], message))]]
        got = {}
        done = run_experts(0, 0, early_full)
        late_full = late.full()
        done = run_experts(1, 0, late_full, (done,))
        in_other = run_combine(0, 1, 1, after=(done,))
        out_other = run_combine(0, 0, 1, after=(in_other,))
        in_total = run_combine(0, 1, 0, sibling(in_other), (out_other,))
        out_total = run_combine(0, 0, 0, sibling(out_other), (in_total,))
        x_pairs.append([x_all[1], sibling(later(x_all[1], in_total))])
        in_parts = [exchange(later(in_total, x_all[1]))]
        done = run_experts(0, 1, early_full, (out_total,))
        done = run_experts(1, 1, late_full, (done,))
        in_other = run_combine(1, 1, 1, after=(done,))
        grads = expert_grads(index, [got[0, m][:4] for m in micros], (in_other,))
        reducing = [Reduce(index, grads)]
        in_total = run_combine(1, 1, 0, sibling(in_other), (grads[0],))
        in_parts.append(exchange(later(in_total, in_parts[0])))
        grads = expert_grads(index, [got[1, m][:4] for m in micros], (in_total,))
        reducing.append(Reduce(index, grads))
        attended_grad = run_hidden_back(0, in_parts[0], (grads[0],))
        query_grad, *parts = run_attend_back(0, attended_grad)
        query_grads, kv_parts, along = [query_grad], [parts], [send_back(parts)]
        attended_grad = run_hidden_back(
            1, in_parts[1], (along[0],) + reducing[0].middle(query_grad)
        )
        out_parts = [exchange(later(out_total, attended_grad))]
        query_grad, *parts = run_attend_back(1, attended_grad)
        query_grads.append(query_grad)
        kv_parts.append(parts)
        along.append(send_back(parts))
        returned = arrive_back(kv_parts[0], along[0])
        out_other = run_combine(1, 0, 1, after=(query_grad, *returned[1:]))
        ends = [reducing[0].end(True, out_other)]
        run_input_back(0, query_grads[0], returned, (along[1], *ends[0]))
        gots = [sibling(ends[0][1])]
        out_total = run_combine(1, 0, 0, sibling(out_other), (backs[0][1],))
        second_shards = output_grads((out_total,))
        outputs[0] = finish_output(0, later(out_parts[0], second_shards[0]))
        step = reducing[1].middle(second_shards[1])
        run_input_back(
            1,
            query_grads[1],
            arrive_back(kv_parts[1], along[1]),
            (second_shards[0], outputs[0], *step),
        )
        out_parts.append(exchange(later(out_total, backs[1][1])))
        second_sum = PlaneSum(second_shards, backs[1][1])
        first_shards = projection_grads((second_sum.reduce.own,))
        second_sum.middle(first_shards[1])
        first_sum = PlaneSum(first_shards, second_sum.reduce.upper)
        second_sum.end(first_sum.reduce.own)
        ends.append(reducing[1].end(True, second_sum.sent[0]))
        step = first_sum.middle(*ends[1])
        gots.append(sibling(ends[1][1]))
        second_sum.over_exp(*step)
        step = first_sum.end(second_sum.sent)
        second_sum.over_exp(*step)
        gate_grad, up_grad, down_grad = unpack(
            index, [e[0] for e in ends], gots, shard, (second_sum.sent,)
        )
        step = first_sum.over_exp(second_sum.sent, gate_grad)
        second_sum.over_exp(*step)
        step = first_sum.over_exp(second_sum.sent)
        second_sum.over_exp(*step)
        step = first_sum.over_exp(second_sum.total)
        outputs[1] = finish_output(1, later(out_parts[1], *step))
        first_sum.over_exp()
        first_total, second_total = first_sum.total, second_sum.total
    else:

        def swap_in(array, axis):
            mine = lax.dynamic_slice_in_dim(array, core * core_experts, core_experts, 0)
            other = lax.dynamic_slice_in_dim(array, (1 - core) * core_experts, core_experts, 0)
            got = sibling(other)
            pair = [jnp.where(core == 0, mine, got), jnp.where(core == 0, got, mine)]
            return jnp.concatenate(pair, axis)

        def swap_out(array, axis):
            half = array.shape[axis] // 2
            mine = lax.dynamic_slice_in_dim(array, core * half, half, axis)
            other = lax.dynamic_slice_in_dim(array, (1 - core) * half, half, axis)
            got = sibling(other.astype(BF)).astype(F32)
            pair = [jnp.where(core == 0, mine, got), jnp.where(core == 0, got, mine)]
            return jnp.concatenate(pair, 0)

        def whole(array):
            blocks = lax.all_gather(array, PLANE)
            return [blocks[j] for j in range(plane)]

        first, second, gain_rows, *rest = project(
            index, tokens, whole(dense), cosine_w, sine_w
        )
        query, normed_in, kv_own = [
            rest[i * micro_count : (i + 1) * micro_count] for i in range(3)
        ]
        weights = [
            jnp.concatenate(gather_chips(later(swap_in(a, axis), first)), axis)
            for a, axis in ((jnp.concatenate([w_gate, w_up], 2), 1), (w_down, 2))
        ]
        kv_blocks, last = [None] * micro_count, first
        gate_up_grad, down_grad = 0.0, 0.0
        group = min(exp_count, 4)
        for m in micros:
            kv_blocks[m] = gather_ctx(later(kv_own[m], last))
            run_attention(m)
            g_all = lax.all_gather(later(message[m : m + 1], last), "exp")
            g_pair = [g_all, sibling(g_all)]
            x_all = lax.all_gather(run_route(m, 1)[0], "exp")
            x_pair = [x_all, sibling(x_all)]
            parts_of = [[], []]
            for g in range(0, exp_count, group):
                runs = range(g, g + group)
                *kept, out, back, sens = experts(
                    index, 0, x_pair, g_pair, 0, runs, weights, (last,)
                )
                gate_up_grad += jnp.einsum(
                    "esd,esf->edf", kept[0], kept[2], preferred_element_type=F32
                )
                down_grad += jnp.einsum("esf,esd->efd", kept[3], kept[1], preferred_element_type=F32)
                for i, source in enumerate((out, back)):
                    sides = [None, None]
                    for side in (1, 0):
                        sides[side] = last = combine(
                            index, side, g_pair[side], 0, runs, [source], [sens] if i else None,
                            sibling(sides[1]) if side == 0 else None, (last,),
                        )
                    parts_of[i].append(last)
            homes = [exchange(jnp.concatenate(parts, 0)) for parts in parts_of]
            outputs[m] = finish_output(m, homes[0])
            last = outputs[m]
            attended_grad = run_hidden_back(m, homes[1])
            query_grad, *parts = run_attend_back(m, attended_grad)
            run_input_back(m, query_grad, [reduce_ctx(parts).astype(BF)])
        gate_up_grad = swap_out(reduce_chips(jnp.split(gate_up_grad.astype(BF), chips, 1)), 1)
        gate_grad, up_grad = gate_up_grad[..., :FF], gate_up_grad[..., FF:]
        down_grad = swap_out(reduce_chips(jnp.split(down_grad.astype(BF), chips, 2)), 2)

        def plane_sum(shards):
            total = jnp.stack(shards, 1)
            total = total.reshape(width, total.shape[-1])
            return lax.psum(lax.psum_scatter(total, PLANE, scatter_dimension=0, tiled=True), "exp")

        first_total, second_total = plane_sum(projection_grads()), plane_sum(output_grads())

    first_total, second_total = first_total.astype(F32), second_total.astype(F32)
    cuts = [H * HD, (H + KVH) * HD, (H + 2 * KVH) * HD]
    query_grad, key_grad, value_grad, norm_one_grad = jnp.split(first_total, cuts, 1)
    return (
        jnp.stack(outputs)[:, None],
        jnp.stack([b[0] for b in backs])[:, None],
        norm_one_grad[:, 0],
        second_total[:, width + EXPERTS],
        query_grad,
        key_grad,
        value_grad,
        second_total[:, :width],
        second_total[:, width : width + EXPERTS],
        gate_grad,
        up_grad,
        down_grad,
    )


def solution(mesh):
    rows = P(None, ("dp", "exp"), "ctx", None)
    row_shard = P(PLANE, None)
    return jax.shard_map(
        on_device,
        mesh=mesh,
        in_specs=(
            rows,
            rows,
            rows,
            P(PLANE),
            P(PLANE),
            row_shard,
            row_shard,
            row_shard,
            row_shard,
            row_shard,
            P("exp", PLANE, None),
            P("exp", PLANE, None),
            P("exp", None, PLANE),
        ),
        out_specs=(
            rows,
            rows,
            P(PLANE),
            P(PLANE),
            row_shard,
            row_shard,
            row_shard,
            row_shard,
            row_shard,
            P("exp", PLANE, None),
            P("exp", PLANE, None),
            P("exp", None, PLANE),
        ),
        check_vma=False,
    )
```
